256 devices in a mesh: ctx: 64 (over z, y, core), tp: 4 (over x).
Axes of the slice: x: 4, y: 4, z: 8, core: 2. Of those that a mesh axis runs over, the one named last changes fastest.
Arguments:
- queries: bfloat16 [512, 8192], P('ctx', 'tp'), may hold values from -100 to 100, as said below
- span_keys: bfloat16 [512, 512], P('ctx', 'tp'), may hold values from -5 to 5
- span_values: bfloat16 [512, 512], P('ctx', 'tp'), may hold values from -24 to 24
- cache_keys: bfloat16 [65536, 512], P('ctx', 'tp'), may hold values from -5 to 5
- stored_values: bfloat16 [65536, 512], P('ctx', 'tp'), may hold values from -24 to 24
- cache_lengths: int32 [64], P('ctx'), may hold values from 256 to 1024, as said below
- span_start: int32 [1], replicated, may hold values from 32768 to 65536
- out_weight: bfloat16 [8192, 16384], P('tp', 'ctx'), may hold values from -0.5 to 0.5
Outputs:
- projected: bfloat16 [512, 16384], P('tp', 'ctx')
The draws below stay inside these ranges and needn't reach their ends.
Inputs may be any that keep to these rules, and one draw needn't show every extreme that they name: `queries`: in some draws a few span tokens are scaled copies of cached keys, so that scores reach about 250 and nearly tie between neighbouring positions. `cache_lengths`: some shard is full in every draw.
All inputs are finite; a program needn't handle non-finite values.
Results may differ from the reference program's by a relative error of at most 0.02.
Values may be sent and summed in bfloat16 or wider, within the bound.
A program may use at most 64 MiB of HBM per device.

```python
import math
import jax
import jax.numpy as jnp
from jax import lax

D = 16384
HEAD_DIMENSION = 128
QUERIES_PER_KV = 16
SPAN_TOKENS = 512
SHARD = 1024
KEY_VALUE_HEADS = 4
QUERY_HEADS = 64
SHARDS = 64
CACHED_POSITIONS = 65536


def base_keys(key):
    return jnp.clip(jax.random.normal(key, (CACHED_POSITIONS, KEY_VALUE_HEADS * HEAD_DIMENSION), jnp.float32), -4.5, 4.5)


def draw_cache_keys(key, part):
    base_offset = base_keys(key)
    return base_offset.astype(jnp.bfloat16)


def draw_queries(key, part):
    key = jax.random.fold_in(key, 7)
    drawn = 1.5 * jnp.clip(jax.random.normal(key, (SPAN_TOKENS, QUERY_HEADS * HEAD_DIMENSION), jnp.float32), -4.5, 4.5)
    return drawn.astype(jnp.bfloat16)


def draw_cache_lengths(key, part):
    key = jax.random.fold_in(key, 3)
    first, second = jax.random.split(key)
    lengths = jax.random.randint(first, (SHARDS,), SHARD // 4, SHARD + 1)
    full_shard = jax.random.randint(second, (), 0, SHARDS)
    return lengths.at[full_shard].set(SHARD).astype(jnp.int32)


def shard_levels(stream_key, dims, cuts, smallest, top_value):
    gain, own = 1.0, jax.random.fold_in(stream_key, 6)
    for dim, shards_of in cuts:
        draws = jnp.exp(jax.random.uniform(jax.random.fold_in(own, dim), (shards_of,), jnp.float32, smallest / len(cuts), top_value / len(cuts)))
        gain = gain * jnp.repeat(draws, dims[dim] // shards_of).reshape([-1 if axis == dim else 1 for axis in range(len(dims))])
    return gain


def gaussian(key, dims, scale, limit, cuts=(), held_as=jnp.bfloat16):
    entries = scale * jax.random.normal(key, dims, jnp.float32)
    if cuts:
        entries = entries * shard_levels(key, dims, cuts, -0.22, 0.18)
    return jnp.clip(entries, -limit, limit).astype(held_as)


def setup_inputs(seed: int = 0) -> dict:
    seeds = jax.random.split(jax.random.key(seed), 9)
    return {
        "queries": draw_queries(jax.random.fold_in(seeds[8], 71), 0),
        "span_keys": gaussian(seeds[1], (SPAN_TOKENS, KEY_VALUE_HEADS * HEAD_DIMENSION), 1.0, 5.0, ((0, 64), (1, 4))),
        "span_values": gaussian(seeds[2], (SPAN_TOKENS, KEY_VALUE_HEADS * HEAD_DIMENSION), 4.0, 24.0, ((0, 64), (1, 4))),
        "cache_keys": draw_cache_keys(jax.random.fold_in(seeds[8], 71), 0),
        "stored_values": gaussian(seeds[4], (CACHED_POSITIONS, KEY_VALUE_HEADS * HEAD_DIMENSION), 4.0, 24.0, ((0, 64), (1, 4))),
        "cache_lengths": draw_cache_lengths(jax.random.fold_in(seeds[8], 71), 0),
        "span_start": jax.random.randint(seeds[6], (1,), CACHED_POSITIONS // 2, CACHED_POSITIONS + 1).astype(jnp.int32),
        "out_weight": gaussian(seeds[7], (QUERY_HEADS * HEAD_DIMENSION, D), HEAD_DIMENSION ** -0.5, 0.5, ((0, 4), (1, 64))),
    }


def attend(query_head, keys_cache, values_cache, keys_new, values_new, visible_cache, causal):
    scale = 1.0 / math.sqrt(HEAD_DIMENSION)
    cache_scores = jnp.dot(query_head, keys_cache.T, preferred_element_type=jnp.float32) * scale
    cache_scores = jnp.where(visible_cache[None, :], cache_scores, -jnp.inf)
    span_scores = jnp.dot(query_head, keys_new.T, preferred_element_type=jnp.float32) * scale
    span_scores = jnp.where(causal, span_scores, -jnp.inf)
    row_max = jnp.maximum(cache_scores.max(axis=1), span_scores.max(axis=1))
    cache_weights = jnp.exp(cache_scores - row_max[:, None])
    span_weights = jnp.exp(span_scores - row_max[:, None])
    totals = cache_weights.sum(axis=1) + span_weights.sum(axis=1)
    numerator = jnp.dot(cache_weights.astype(jnp.bfloat16), values_cache, preferred_element_type=jnp.float32)
    numerator = numerator + jnp.dot(span_weights.astype(jnp.bfloat16), values_new, preferred_element_type=jnp.float32)
    return (numerator / totals[:, None]).astype(jnp.bfloat16)

def split_heads(input_array, element_count):
    return input_array.reshape(element_count, KEY_VALUE_HEADS, HEAD_DIMENSION).transpose(1, 0, 2)

def reference(queries, span_keys, span_values, cache_keys, stored_values, cache_lengths, span_start, out_weight):
    positions = jnp.arange(CACHED_POSITIONS, dtype=jnp.int32)
    shard_of = (positions // SHARD).astype(jnp.int32)
    live = positions % SHARD < cache_lengths[shard_of]
    visible_cache = live & (positions < span_start[0])
    token_ids = jnp.arange(SPAN_TOKENS, dtype=jnp.int32)
    causal = token_ids[None, :] <= token_ids[:, None]
    query_head_count = queries.reshape(SPAN_TOKENS, KEY_VALUE_HEADS, QUERIES_PER_KV, HEAD_DIMENSION).transpose(1, 2, 0, 3)

    def per_group(inputs):
        group_queries, keys_cache, values_cache, keys_new, values_new = inputs

        def per_head(query_head):
            return attend(query_head, keys_cache, values_cache, keys_new, values_new, visible_cache, causal)
        return lax.map(per_head, group_queries)
    attended = lax.map(per_group, (query_head_count, split_heads(cache_keys, CACHED_POSITIONS), split_heads(stored_values, CACHED_POSITIONS), split_heads(span_keys, SPAN_TOKENS), split_heads(span_values, SPAN_TOKENS)))
    attended = attended.transpose(2, 0, 1, 3).reshape(SPAN_TOKENS, QUERY_HEADS * HEAD_DIMENSION)
    return jnp.dot(attended, out_weight, preferred_element_type=jnp.float32).astype(jnp.bfloat16)
```

```python
import functools
import math

import jax
import jax.numpy as jnp
from jax import lax
from jax.experimental import pallas as pl
from jax.experimental.pallas import tpu as pltpu
from jax.sharding import PartitionSpec as P

MESH = pl.DeviceIdType.MESH
F32, BF16 = jnp.float32, jnp.bfloat16
NX, NY, NZ, CORES = 4, 4, 8, 2
HD = 128
TOK = 8
SHARD = 1024
CHUNKS = 4
HL = 8 // CHUNKS
L = HL * HD
SPAN_PAD = 128
KEYS = CORES * SHARD + SPAN_PAD
COLS = 256
DEAD = -1e30
SCALE = math.log2(math.e) / math.sqrt(HD)
Y_ORDER = (1, 3, 2)


def nt(a, b):
    return lax.dot_general(a, b, (((1,), (1,)), ((), ())), preferred_element_type=F32)


def nn(a, b):
    return jnp.dot(a, b, preferred_element_type=F32)


def kernel(
    q_ref, sk_ref, sv_ref, len_ref, start_ref, ck_ref, cv_ref, w_ref, out_ref,
    kraw, vraw, span, keys, vals, weight, qg, ob, st, on, sn, nz, nr, ag, terms, tb, tr,
    loc, bar_s, bar_r, qz_s, qz_r, qy_s, qy_r, ny_s, ny_r, ns_s, ns_r, nz_s, nz_r,
    az_s, az_r, ay_s, ay_r, rx_s, rx_r,
):
    ctx = lax.axis_index("ctx")
    x = lax.axis_index("tp")
    c = ctx % 2
    y = (ctx // 2) % NY
    z = ctx // (2 * NY)
    chip = z * NY + y

    def dev(dx, dy, dz, dc):
        return ((((z + dz % NZ) % NZ) * NY + (y + dy % NY) % NY) * 2 + (c + dc) % 2, (x + dx % NX) % NX)

    def rc(src, dst, ss, rs, to):
        return pltpu.make_async_remote_copy(
            src_ref=src, dst_ref=dst, send_sem=ss, recv_sem=rs, device_id=to, device_id_type=MESH
        )

    lk = pltpu.make_async_copy(ck_ref, kraw, loc.at[0])
    lv = pltpu.make_async_copy(cv_ref, vraw, loc.at[1])
    lw = pltpu.make_async_copy(w_ref, weight.at[0], loc.at[2])
    lk.start()
    lv.start()
    lw.start()

    peers = [dev(0, 0, 0, 1)]
    peers += [dev(0, d, 0, 0) for d in range(1, NY)]
    peers += [dev(0, 0, d, 0) for d in range(1, NZ)]
    peers += [dev(d, 0, 0, e) for d in range(1, NX) for e in range(2)]
    barrier = pltpu.get_barrier_semaphore()
    for p in peers:
        pl.semaphore_signal(barrier, inc=1, device_id=p, device_id_type=MESH)

    qf = q_ref[...].astype(F32)
    qf = jnp.concatenate([qf[:, : 8 * HD], qf[:, 8 * HD :]], axis=0).astype(BF16)
    for ci in range(CHUNKS):
        qg[ci, 0, 0] = qf[:, ci * L : (ci + 1) * L]
    span[0] = jnp.concatenate([sk_ref[...].astype(F32), sv_ref[...].astype(F32)], axis=0).astype(BF16)
    pl.semaphore_wait(barrier, len(peers))

    def qz(ci, d):
        return rc(qg.at[ci, 0, 0], qg.at[ci, 0, d], qz_s.at[ci, d], qz_r.at[ci, d], dev(0, 0, d, 0))

    def qy(ci, d):
        return rc(qg.at[ci, 0], qg.at[ci, d], qy_s.at[ci, d], qy_r.at[ci, d], dev(0, d, 0, 0))

    for ci in range(CHUNKS):
        for d in range(1, NZ):
            qz(ci, d).start()

    sib = dev(0, 0, 0, 1)
    own_rows = pl.ds(pl.multiple_of(c * SHARD, SHARD), SHARD)
    csp = rc(span.at[0], span.at[1], bar_s.at[0], bar_r.at[0], sib)
    csp.start()
    begin = start_ref[0]
    row = lax.broadcasted_iota(jnp.int32, (SHARD, HD), 0)
    live = (row < len_ref[0]) & (row + ctx * SHARD < begin)
    lk.wait()
    kr = kraw[...]
    keys[own_rows] = jnp.where(live, kr.astype(F32), kr[0:1].astype(F32)).astype(BF16)
    ck = rc(keys.at[own_rows], keys.at[own_rows], bar_s.at[1], bar_r.at[1], sib)
    ck.start()
    lv.wait()
    vals[own_rows, 0:HD] = jnp.where(live, vraw[...].astype(F32), 0.0).astype(BF16)
    vals[own_rows, HD:] = jnp.where(live, 1.0, 0.0).astype(BF16)
    cv = rc(vals.at[own_rows], vals.at[own_rows], bar_s.at[2], bar_r.at[2], sib)
    cv.start()
    lw.wait()
    cw = rc(weight.at[0], weight.at[1], bar_s.at[3], bar_r.at[3], sib)
    cw.start()
    csp.wait_recv()
    s_own = span[0].astype(F32)
    s_sib = span[1].astype(F32)
    first = jnp.where(c == 0, s_own, s_sib)
    second = jnp.where(c == 0, s_sib, s_own)
    base = CORES * SHARD
    keys[base : base + 16] = jnp.concatenate([first[0:8], second[0:8]], axis=0).astype(BF16)
    keys[base + 16 : KEYS] = jnp.zeros((SPAN_PAD - 16, HD), BF16)
    vals[base : base + 16, 0:HD] = jnp.concatenate([first[8:16], second[8:16]], axis=0).astype(BF16)
    vals[base : base + 16, HD:] = jnp.ones((16, HD), BF16)
    vals[base + 16 : KEYS] = jnp.zeros((SPAN_PAD - 16, 2 * HD), BF16)

    for ci in range(CHUNKS):
        for d in range(1, NZ):
            qz(ci, d).wait_recv()
        for d in Y_ORDER:
            qy(ci, d).start()
    ck.wait_recv()
    cv.wait_recv()

    even_live = chip * (2 * SHARD) < begin
    odd_live = chip * (2 * SHARD) + SHARD < begin
    c0 = jnp.where(even_live, SCALE, 0.0).astype(F32)
    b0 = jnp.where(even_live, 0.0, DEAD).astype(F32)
    c1 = jnp.where(odd_live, SCALE, 0.0).astype(F32)
    b1 = jnp.where(odd_live, 0.0, DEAD).astype(F32)
    rows_i = lax.broadcasted_iota(jnp.int32, (2 * HD, SPAN_PAD), 0)
    cols_i = lax.broadcasted_iota(jnp.int32, (2 * HD, SPAN_PAD), 1)
    lane8 = lax.broadcasted_iota(jnp.int32, (TOK, HD), 1)
    lane16 = lax.broadcasted_iota(jnp.int32, (2 * TOK, HD), 1)

    def ny(ci, d):
        return rc(ob.at[ci, d], on.at[ci, d], ny_s.at[ci, d], ny_r.at[ci, d], dev(0, -d, 0, 0))

    def ns(ci, d):
        return rc(st.at[ci, d], sn.at[ci, d], ns_s.at[ci, d], ns_r.at[ci, d], dev(0, -d, 0, 0))

    def attend(ci, yd):
        qa = qg[ci, yd]
        q2 = jnp.concatenate([qa[:, :, i * HD : (i + 1) * HD].reshape(HD, HD) for i in range(HL)], axis=0)
        s0 = nt(q2, keys[0:SHARD])
        s1 = nt(q2, keys[SHARD : 2 * SHARD])
        ss = nt(q2, keys[base:KEYS]) * SCALE
        owner_z = (z + NZ - ((rows_i & (HD - 1)) >> 4)) & (NZ - 1)
        owner_y = (y + NY - yd) & (NY - 1)
        token = (owner_z * NY + owner_y) * 16 + c * 8 + (rows_i & 7)
        ss = jnp.where((cols_i < 16) & (chip * 16 + cols_i <= token), ss, 2 * DEAD)
        m0 = jnp.max(s0, axis=1, keepdims=True) * c0 + b0
        m1 = jnp.max(s1, axis=1, keepdims=True) * c1 + b1
        ms = jnp.max(ss, axis=1, keepdims=True)
        m = jnp.maximum(jnp.maximum(jnp.maximum(m0, m1), ms), DEAD)
        p0 = jnp.exp2(s0 * c0 + (b0 - m)).astype(BF16)
        p1 = jnp.exp2(s1 * c1 + (b1 - m)).astype(BF16)
        ps = jnp.exp2(ss - m).astype(BF16)
        acc = nn(p0, vals[0:SHARD]) + nn(p1, vals[SHARD : 2 * SHARD]) + nn(ps, vals[base:KEYS])
        total = jnp.maximum(acc[:, HD:], 1e-30)
        o = (acc[:, :HD] / total).astype(BF16)
        lse = m + jnp.log2(total)
        tile = jnp.zeros((TOK, HD), F32)
        for i in range(HL):
            ob[ci, yd, :, :, i * HD : (i + 1) * HD] = o[i * HD : (i + 1) * HD].reshape(NZ, 16, HD)
            for zd in range(NZ):
                for hh in range(2):
                    r = i * HD + zd * 16 + hh * 8
                    tile = jnp.where(lane8 == zd * 16 + i * 2 + hh, lse[r : r + 8], tile)
        st[ci, yd] = tile

    def step(s, carry):
        far = s >= CHUNKS
        t = jnp.where(far, s - CHUNKS, 0)
        ci = jnp.where(far, t // 3, s)
        k = t % 3
        yd = jnp.where(far, jnp.where(k == 0, Y_ORDER[0], jnp.where(k == 1, Y_ORDER[1], Y_ORDER[2])), 0)
        for d in range(1, NY):

            @pl.when(yd == d)
            def _():
                qy(ci, d).wait_recv()

        attend(ci, yd)
        for d in range(1, NY):

            @pl.when(yd == d)
            def _():
                ny(ci, d).start()
                ns(ci, d).start()

        return carry

    lax.fori_loop(0, CHUNKS * NY, step, 0)

    def nzc(ci, d):
        return rc(nz.at[ci, d], nr.at[ci, d], nz_s.at[ci, d], nz_r.at[ci, d], dev(0, 0, -d, 0))

    def az(ci, d):
        return rc(ag.at[ci, 0, 0], ag.at[ci, 0, d], az_s.at[ci, d], az_r.at[ci, d], dev(0, 0, d, 0))

    def ay(ci, d):
        return rc(ag.at[ci, 0], ag.at[ci, d], ay_s.at[ci, d], ay_r.at[ci, d], dev(0, d, 0, 0))

    def merge(parts):
        top = functools.reduce(jnp.maximum, [lse for lse, _ in parts])
        ws = [jnp.exp2(lse - top) for lse, _ in parts]
        total = functools.reduce(jnp.add, ws)
        num = functools.reduce(jnp.add, [w * o.astype(F32) for w, (_, o) in zip(ws, parts)])
        return num / total, top + jnp.log2(total)

    def reduce_y(ci):
        for d in range(1, NY):
            ny(ci, d).wait_recv()
            ns(ci, d).wait_recv()
        tiles = [st[ci, 0]] + [sn[ci, d] for d in range(1, NY)]
        for zd in range(NZ):
            stat = jnp.zeros((16, HD), F32)
            for i in range(HL):
                parts = []
                for d in range(NY):
                    k = zd * 16 + i * 2
                    lse = jnp.concatenate(
                        [jnp.broadcast_to(tiles[d][:, k + hh : k + hh + 1], (8, HD)) for hh in range(2)], axis=0
                    )
                    src = ob if d == 0 else on
                    parts.append((lse, src[ci, d, zd, :, i * HD : (i + 1) * HD]))
                o, lse = merge(parts)
                nz[ci, zd, :, i * HD : (i + 1) * HD] = o.astype(BF16)
                hi = lse.astype(BF16).astype(F32)
                mid = (lse - hi).astype(BF16).astype(F32)
                lo = lse - hi - mid
                for p, v in enumerate((hi, mid, lo)):
                    stat = jnp.where(lane16 == i * 4 + p, v, stat)
            nz[ci, zd, :, L:] = stat.astype(BF16)
        for d in range(1, NZ):
            nzc(ci, d).start()

    def reduce_z(ci):
        for d in range(1, NZ):
            nzc(ci, d).wait_recv()
        for i in range(HL):
            parts = []
            for d in range(NZ):
                src = nz if d == 0 else nr
                stat = src[ci, d, :, L:].astype(F32)
                pick = (lane16 >= i * 4) & (lane16 < i * 4 + 3)
                lse = jnp.broadcast_to(jnp.sum(jnp.where(pick, stat, 0.0), axis=1, keepdims=True), (16, HD))
                parts.append((lse, src[ci, d, :, i * HD : (i + 1) * HD]))
            o, _ = merge(parts)
            ag[ci, 0, 0, :, i * HD : (i + 1) * HD] = o.astype(BF16)
        for d in range(1, NZ):
            az(ci, d).start()

    def spread_y(ci):
        for d in range(1, NZ):
            az(ci, d).wait_recv()
        for d in Y_ORDER:
            ay(ci, d).start()

    terms[...] = jnp.zeros_like(terms)

    def project(ci):
        for d in range(1, NY):
            ay(ci, d).wait_recv()
        a = ag[ci].astype(F32).reshape(NY * NZ, 16, L)
        for hh in range(2):
            ah = a[:, hh * 8 : (hh + 1) * 8].reshape(NY * NZ * TOK, L).astype(BF16)
            rows = pl.ds(pl.multiple_of(hh * 8 * HD + ci * L, L), L)
            for e in range(2):
                terms[e] += nn(ah, weight[e, rows])

    def tail(t, carry):
        @pl.when(t < CHUNKS)
        def _():
            reduce_y(t)

        @pl.when((t >= 1) & (t < CHUNKS + 1))
        def _():
            reduce_z(t - 1)

        @pl.when((t >= 2) & (t < CHUNKS + 2))
        def _():
            spread_y(t - 2)

        return carry

    lax.fori_loop(0, CHUNKS + 2, tail, 0)
    cw.wait_recv()

    def proj_step(t, carry):
        project(t)
        return carry

    lax.fori_loop(0, CHUNKS, proj_step, 0)

    def place(zz, carry):
        zd = (z + NZ - zz) % NZ
        for e in range(2):
            parts = []
            for yy in range(NY):
                yd = (y + NY - yy) % NY
                parts.append(terms[e, pl.ds(pl.multiple_of((yd * NZ + zd) * TOK, TOK), TOK)])
            tb[e, zz] = jnp.concatenate(parts, axis=0).astype(BF16)
        return carry

    lax.fori_loop(0, NZ, place, 0)
    ZX = NZ // NX

    def rx(dx, e):
        to = (x + dx) % NX
        return rc(tb.at[e, pl.ds(to * ZX, ZX)], tr.at[e, dx], rx_s.at[e, dx], rx_r.at[e, dx], dev(dx, 0, 0, e))

    for dx in range(1, NX):
        for e in range(2):
            rx(dx, e).start()
    rx(0, 1).start()
    sums = [tb[0, pl.ds(x * ZX, ZX)].astype(F32), None]
    rx(0, 1).wait_recv()
    sums[1] = tr[1, 0].astype(F32)
    for dx in range(1, NX):
        for e in range(2):
            rx(dx, e).wait_recv()
            sums[e] = sums[e] + tr[e, dx].astype(F32)
    low = jnp.where(c == 0, sums[0], sums[1]).reshape(ZX * NY, 1, TOK, COLS)
    high = jnp.where(c == 0, sums[1], sums[0]).reshape(ZX * NY, 1, TOK, COLS)
    out_ref[...] = jnp.concatenate([low, high], axis=1).reshape(ZX * NY * 2 * TOK, COLS).astype(BF16)

    csp.wait_send()
    ck.wait_send()
    cv.wait_send()
    cw.wait_send()

    def drain(ci, carry):
        for d in range(1, NZ):
            qz(ci, d).wait_send()
            nzc(ci, d).wait_send()
            az(ci, d).wait_send()
        for d in range(1, NY):
            qy(ci, d).wait_send()
            ny(ci, d).wait_send()
            ns(ci, d).wait_send()
            ay(ci, d).wait_send()
        return carry

    lax.fori_loop(0, CHUNKS, drain, 0)
    rx(0, 1).wait_send()
    for dx in range(1, NX):
        for e in range(2):
            rx(dx, e).wait_send()


def device_step(queries, span_keys, span_values, cache_keys, stored_values, cache_lengths, span_start, out_weight):
    vm = pl.BlockSpec(memory_space=pltpu.VMEM)
    sm = pl.BlockSpec(memory_space=pltpu.SMEM)
    hbm = pl.BlockSpec(memory_space=pl.ANY)
    dma = pltpu.SemaphoreType.DMA
    rows = 16
    scratch = [
        pltpu.VMEM((SHARD, HD), BF16),
        pltpu.VMEM((SHARD, HD), BF16),
        pltpu.VMEM((2, 16, HD), BF16),
        pltpu.VMEM((KEYS, HD), BF16),
        pltpu.VMEM((KEYS, 2 * HD), BF16),
        pltpu.VMEM((2, 16 * HD, COLS), BF16),
        pltpu.VMEM((CHUNKS, NY, NZ, rows, L), BF16),
        pltpu.VMEM((CHUNKS, NY, NZ, rows, L), BF16),
        pltpu.VMEM((CHUNKS, NY, TOK, HD), F32),
        pltpu.VMEM((CHUNKS, NY, NZ, rows, L), BF16),
        pltpu.VMEM((CHUNKS, NY, TOK, HD), F32),
        pltpu.VMEM((CHUNKS, NZ, rows, L + HD), BF16),
        pltpu.VMEM((CHUNKS, NZ, rows, L + HD), BF16),
        pltpu.VMEM((CHUNKS, NY, NZ, rows, L), BF16),
        pltpu.VMEM((2, NY * NZ * TOK, COLS), F32),
        pltpu.VMEM((2, NZ, NY * TOK, COLS), BF16),
        pltpu.VMEM((2, NX, NZ // NX, NY * TOK, COLS), BF16),
        dma((3,)),
        dma((4,)),
        dma((4,)),
        dma((CHUNKS, NZ)),
        dma((CHUNKS, NZ)),
        dma((CHUNKS, NY)),
        dma((CHUNKS, NY)),
        dma((CHUNKS, NY)),
        dma((CHUNKS, NY)),
        dma((CHUNKS, NY)),
        dma((CHUNKS, NY)),
        dma((CHUNKS, NZ)),
        dma((CHUNKS, NZ)),
        dma((CHUNKS, NZ)),
        dma((CHUNKS, NZ)),
        dma((CHUNKS, NY)),
        dma((CHUNKS, NY)),
        dma((2, NX)),
        dma((2, NX)),
    ]
    return pl.pallas_call(
        kernel,
        out_shape=jax.ShapeDtypeStruct((NZ // NX * NY * 2 * TOK, COLS), BF16),
        in_specs=[vm, vm, vm, sm, sm, hbm, hbm, hbm],
        out_specs=vm,
        scratch_shapes=scratch,
        compiler_params=pltpu.CompilerParams(
            collective_id=0, has_side_effects=True, vmem_limit_bytes=48 << 20
        ),
    )(queries, span_keys, span_values, cache_lengths, span_start, cache_keys, stored_values, out_weight)


def solution(mesh):
    return jax.shard_map(
        device_step,
        mesh=mesh,
        in_specs=(
            P("ctx", "tp"),
            P("ctx", "tp"),
            P("ctx", "tp"),
            P("ctx", "tp"),
            P("ctx", "tp"),
            P("ctx"),
            P(),
            P("tp", "ctx"),
        ),
        out_specs=P("tp", "ctx"),
        check_vma=False,
    )
```

```python
import functools
import math

import jax
import jax.numpy as jnp
from jax import lax
from jax.experimental import pallas as pl
from jax.experimental.pallas import tpu as pltpu
from jax.sharding import PartitionSpec as P

MESH = pl.DeviceIdType.MESH
F32, BF16 = jnp.float32, jnp.bfloat16
NX, NY, NZ, CORES = 4, 4, 8, 2
HD = 128
TOK = 8
SHARD = 1024
CHUNKS = 4
HL = 8 // CHUNKS
L = HL * HD
SPAN_PAD = 128
KEYS = CORES * SHARD + SPAN_PAD
COLS = 256
DEAD = -1e30
SCALE = math.log2(math.e) / math.sqrt(HD)
Y_ORDER = (1, 3, 2)
KB = 512
NEAR = CHUNKS // 2
FAR = 3 if CHUNKS == 4 else 1
LAG = 2 if CHUNKS == 4 else 1


def nt(a, b):
    return lax.dot_general(a, b, (((1,), (1,)), ((), ())), preferred_element_type=F32)


def nn(a, b):
    return jnp.dot(a, b, preferred_element_type=F32)


def kernel(
    q_ref, sk_ref, sv_ref, len_ref, start_ref, ck_ref, cv_ref, w_ref, out_ref,
    qraw, skraw, svraw, kraw, vraw, span, keys, vals, weight, qg, ob, st, on, sn, nz, nr, ag, terms, tb, tr,
    loc, bar_s, bar_r, qz_s, qz_r, qy_s, qy_r, ny_s, ny_r, ns_s, ns_r, nz_s, nz_r,
    az_s, az_r, ay_s, ay_r, rx_s, rx_r,
):
    ctx = lax.axis_index("ctx")
    x = lax.axis_index("tp")
    c = ctx % 2
    y = (ctx // 2) % NY
    z = ctx // (2 * NY)
    chip = z * NY + y

    def dev(dx, dy, dz, dc):
        return ((((z + dz % NZ) % NZ) * NY + (y + dy % NY) % NY) * 2 + (c + dc) % 2, (x + dx % NX) % NX)

    def rc(src, dst, ss, rs, to):
        return pltpu.make_async_remote_copy(
            src_ref=src, dst_ref=dst, send_sem=ss, recv_sem=rs, device_id=to, device_id_type=MESH
        )

    lk = pltpu.make_async_copy(ck_ref, kraw, loc.at[0])
    lv = pltpu.make_async_copy(cv_ref, vraw, loc.at[1])
    lw = pltpu.make_async_copy(w_ref, weight.at[0], loc.at[2])
    small = [
        pltpu.make_async_copy(a, b, loc.at[3 + i])
        for i, (a, b) in enumerate(
            ((q_ref, qraw), (sk_ref, skraw), (sv_ref, svraw))
        )
    ]
    for cp in small:
        cp.start()
    lk.start()
    lv.start()
    lw.start()

    peers = [dev(0, 0, 0, 1)]
    peers += [dev(0, d, 0, 0) for d in range(1, NY)]
    peers += [dev(0, 0, d, 0) for d in range(1, NZ)]
    peers += [dev(d, 0, 0, e) for d in range(1, NX) for e in range(2)]
    barrier = pltpu.get_barrier_semaphore()
    for p in peers:
        pl.semaphore_signal(barrier, inc=1, device_id=p, device_id_type=MESH)

    for cp in small:
        cp.wait()
    qf = qraw[...].astype(F32)
    qf = jnp.concatenate([qf[:, : 8 * HD], qf[:, 8 * HD :]], axis=0).astype(BF16)
    for ci in range(CHUNKS):
        qg[ci, 0, 0] = qf[:, ci * L : (ci + 1) * L]
    span[0] = jnp.concatenate([skraw[...].astype(F32), svraw[...].astype(F32)], axis=0).astype(BF16)

    def qz(ci, d):
        return rc(qg.at[ci, 0, 0], qg.at[ci, 0, d], qz_s.at[ci, d], qz_r.at[ci, d], dev(0, 0, d, 0))

    def qy(ci, d):
        return rc(qg.at[ci, 0], qg.at[ci, d], qy_s.at[ci, d], qy_r.at[ci, d], dev(0, d, 0, 0))

    sib = dev(0, 0, 0, 1)
    own_rows = pl.ds(pl.multiple_of(c * SHARD, SHARD), SHARD)
    csp = rc(span.at[0], span.at[1], bar_s.at[0], bar_r.at[0], sib)
    ck = rc(keys.at[own_rows], keys.at[own_rows], bar_s.at[1], bar_r.at[1], sib)
    cv = rc(vals.at[own_rows], vals.at[own_rows], bar_s.at[2], bar_r.at[2], sib)
    cw = rc(weight.at[0], weight.at[1], bar_s.at[3], bar_r.at[3], sib)
    begin = start_ref[0]
    row = lax.broadcasted_iota(jnp.int32, (SHARD, HD), 0)
    live = (row < len_ref[0]) & (row + ctx * SHARD < begin)
    lk.wait()
    kr = kraw[...]
    keys[own_rows] = jnp.where(live, kr.astype(F32), kr[0:1].astype(F32)).astype(BF16)
    lv.wait()
    vals[own_rows, 0:HD] = jnp.where(live, vraw[...].astype(F32), 0.0).astype(BF16)
    vals[own_rows, HD:] = jnp.where(live, 1.0, 0.0).astype(BF16)
    pl.semaphore_wait(barrier, len(peers))
    for ci in range(CHUNKS):
        for d in range(1, NZ):
            qz(ci, d).start()
    csp.start()
    ck.start()
    cv.start()
    lw.wait()
    cw.start()
    csp.wait_recv()
    s_own = span[0].astype(F32)
    s_sib = span[1].astype(F32)
    first = jnp.where(c == 0, s_own, s_sib)
    second = jnp.where(c == 0, s_sib, s_own)
    base = CORES * SHARD
    keys[base : base + 16] = jnp.concatenate([first[0:8], second[0:8]], axis=0).astype(BF16)
    keys[base + 16 : KEYS] = jnp.zeros((SPAN_PAD - 16, HD), BF16)
    vals[base : base + 16, 0:HD] = jnp.concatenate([first[8:16], second[8:16]], axis=0).astype(BF16)
    vals[base : base + 16, HD:] = jnp.ones((16, HD), BF16)
    vals[base + 16 : KEYS] = jnp.zeros((SPAN_PAD - 16, 2 * HD), BF16)

    even_live = chip * (2 * SHARD) < begin
    odd_live = chip * (2 * SHARD) + SHARD < begin
    c0 = jnp.where(even_live, SCALE, 0.0).astype(F32)
    b0 = jnp.where(even_live, 0.0, DEAD).astype(F32)
    c1 = jnp.where(odd_live, SCALE, 0.0).astype(F32)
    b1 = jnp.where(odd_live, 0.0, DEAD).astype(F32)
    lane8 = lax.broadcasted_iota(jnp.int32, (TOK, HD), 1)
    lane16 = lax.broadcasted_iota(jnp.int32, (2 * TOK, HD), 1)

    def ny(ci, d):
        return rc(ob.at[ci, d], on.at[ci, d], ny_s.at[ci, d], ny_r.at[ci, d], dev(0, -d, 0, 0))

    def ns(ci, d):
        return rc(st.at[ci, d], sn.at[ci, d], ns_s.at[ci, d], ns_r.at[ci, d], dev(0, -d, 0, 0))

    def attend(pairs):
        m_rows = len(pairs) * HL * HD
        rows_i = lax.broadcasted_iota(jnp.int32, (HD, SPAN_PAD), 0)
        cols_i = lax.broadcasted_iota(jnp.int32, (HD, SPAN_PAD), 1)
        owner_z = (z + NZ - (rows_i >> 4)) & (NZ - 1)
        blocks, masks = [], []
        for ci, yd in pairs:
            qa = qg[ci, yd]
            token = (owner_z * NY + ((y + NY - yd) & (NY - 1))) * 16 + c * 8 + (rows_i & 7)
            see = (cols_i < 16) & (chip * 16 + cols_i <= token)
            for i in range(HL):
                blocks.append(qa[:, :, i * HD : (i + 1) * HD].reshape(HD, HD))
                masks.append(jnp.where(see, 0.0, 2 * DEAD))
        q2 = jnp.concatenate(blocks, axis=0)
        ss = nt(q2, keys[base:KEYS]) * SCALE + jnp.concatenate(masks, axis=0)
        m = jnp.maximum(jnp.broadcast_to(jnp.max(ss, axis=1, keepdims=True), (m_rows, HD)), DEAD)
        acc = nn(jnp.exp2(ss - m).astype(BF16), vals[base:KEYS])
        for kb in range(0, CORES * SHARD, KB):
            cs, bs = (c0, b0) if kb < SHARD else (c1, b1)
            s = nt(q2, keys[kb : kb + KB])
            top = functools.reduce(jnp.maximum, [s[:, j : j + HD] for j in range(0, KB, HD)])
            top = jnp.broadcast_to(jnp.max(top, axis=1, keepdims=True), (m_rows, HD)) * cs + bs
            new = jnp.maximum(m, top)
            keep = jnp.exp2(m - new)
            off = bs - new
            p = jnp.concatenate(
                [jnp.exp2(s[:, j : j + HD] * cs + off).astype(BF16) for j in range(0, KB, HD)], axis=1
            )
            acc = acc * jnp.concatenate([keep, keep], axis=1) + nn(p, vals[kb : kb + KB])
            m = new
        total = jnp.maximum(acc[:, HD:], 1e-30)
        o = (acc[:, :HD] / total).astype(BF16)
        lse = m + jnp.log2(total)
        for b, (ci, yd) in enumerate(pairs):
            tile = jnp.zeros((TOK, HD), F32)
            for i in range(HL):
                r = (b * HL + i) * HD
                ob[ci, yd, :, :, i * HD : (i + 1) * HD] = o[r : r + HD].reshape(NZ, 16, HD)
                for zd in range(NZ):
                    for hh in range(2):
                        w = r + zd * 16 + hh * 8
                        tile = jnp.where(lane8 == zd * 16 + i * 2 + hh, lse[w : w + 8], tile)
            st[ci, yd] = tile

    def nzc(ci, d):
        return rc(nz.at[ci, d], nr.at[ci, d], nz_s.at[ci, d], nz_r.at[ci, d], dev(0, 0, -d, 0))

    def az(ci, d):
        return rc(ag.at[ci, 0, 0], ag.at[ci, 0, d], az_s.at[ci, d], az_r.at[ci, d], dev(0, 0, d, 0))

    def ay(ci, d):
        return rc(ag.at[ci, 0], ag.at[ci, d], ay_s.at[ci, d], ay_r.at[ci, d], dev(0, d, 0, 0))

    def merge(parts):
        top = functools.reduce(jnp.maximum, [lse for lse, _ in parts])
        ws = [jnp.exp2(lse - top) for lse, _ in parts]
        total = functools.reduce(jnp.add, ws)
        num = functools.reduce(jnp.add, [w * o.astype(F32) for w, (_, o) in zip(ws, parts)])
        return num / total, top + jnp.log2(total)

    def reduce_y(ci):
        for d in range(1, NY):
            ny(ci, d).wait_recv()
            ns(ci, d).wait_recv()
        tiles = [st[ci, 0]] + [sn[ci, d] for d in range(1, NY)]
        for zd in range(NZ):
            stat = jnp.zeros((16, HD), F32)
            for i in range(HL):
                parts = []
                for d in range(NY):
                    k = zd * 16 + i * 2
                    lse = jnp.concatenate(
                        [jnp.broadcast_to(tiles[d][:, k + hh : k + hh + 1], (8, HD)) for hh in range(2)], axis=0
                    )
                    src = ob if d == 0 else on
                    parts.append((lse, src[ci, d, zd, :, i * HD : (i + 1) * HD]))
                o, lse = merge(parts)
                nz[ci, zd, :, i * HD : (i + 1) * HD] = o.astype(BF16)
                hi = lse.astype(BF16).astype(F32)
                mid = (lse - hi).astype(BF16).astype(F32)
                lo = lse - hi - mid
                for p, v in enumerate((hi, mid, lo)):
                    stat = jnp.where(lane16 == i * 4 + p, v, stat)
            nz[ci, zd, :, L:] = stat.astype(BF16)
        for d in range(1, NZ):
            nzc(ci, d).start()

    def reduce_z(ci):
        for d in range(1, NZ):
            nzc(ci, d).wait_recv()
        for i in range(HL):
            parts = []
            for d in range(NZ):
                src = nz if d == 0 else nr
                stat = src[ci, d, :, L:].astype(F32)
                pick = (lane16 >= i * 4) & (lane16 < i * 4 + 3)
                lse = jnp.broadcast_to(jnp.sum(jnp.where(pick, stat, 0.0), axis=1, keepdims=True), (16, HD))
                parts.append((lse, src[ci, d, :, i * HD : (i + 1) * HD]))
            o, _ = merge(parts)
            ag[ci, 0, 0, :, i * HD : (i + 1) * HD] = o.astype(BF16)
        for d in range(1, NZ):
            az(ci, d).start()

    def spread_y(ci):
        for d in range(1, NZ):
            az(ci, d).wait_recv()
        for d in Y_ORDER:
            ay(ci, d).start()

    terms[...] = jnp.zeros_like(terms)

    def project(ci):
        for d in range(1, NY):
            ay(ci, d).wait_recv()
        a = ag[ci].astype(F32).reshape(NY * NZ, 16, L)
        for hh in range(2):
            ah = a[:, hh * 8 : (hh + 1) * 8].reshape(NY * NZ * TOK, L).astype(BF16)
            rows = pl.ds(pl.multiple_of(hh * 8 * HD + ci * L, L), L)
            for e in range(2):
                terms[e] += nn(ah, weight[e, rows])

    def near(t, carry):
        for u in range(NEAR):
            ci = t * NEAR + u
            for d in range(1, NZ):
                qz(ci, d).wait_recv()
            for d in Y_ORDER:
                qy(ci, d).start()

        @pl.when(t == 0)
        def _():
            ck.wait_recv()
            cv.wait_recv()

        attend([(t * NEAR + u, 0) for u in range(NEAR)])
        return carry

    lax.fori_loop(0, CHUNKS // NEAR, near, 0)

    groups = 3 // FAR

    def far(s, carry):
        t, k = s // groups, s % groups
        if FAR == 3:
            cols = list(Y_ORDER)
        else:
            cols = [jnp.where(k == 0, Y_ORDER[0], jnp.where(k == 1, Y_ORDER[1], Y_ORDER[2]))]
        for g in range(groups):

            @pl.when(k == g)
            def _():
                for d in Y_ORDER[g * FAR : (g + 1) * FAR]:
                    qy(t, d).wait_recv()

        attend([(t, d) for d in cols])
        for g in range(groups):

            @pl.when(k == g)
            def _():
                for d in Y_ORDER[g * FAR : (g + 1) * FAR]:
                    ny(t, d).start()
                    ns(t, d).start()

        @pl.when((t >= LAG) & (k == groups - 1))
        def _():
            reduce_y(t - LAG)

        return carry

    lax.fori_loop(0, CHUNKS * groups, far, 0)
    cw.wait_recv()

    def tail(u, carry):
        @pl.when(u < CHUNKS)
        def _():
            reduce_z(u)

        @pl.when(u < LAG)
        def _():
            reduce_y(u + CHUNKS - LAG)

        @pl.when((u >= 1) & (u < CHUNKS + 1))
        def _():
            spread_y(u - 1)

        @pl.when(u >= CHUNKS)
        def _():
            project(u - CHUNKS)

        return carry

    lax.fori_loop(0, 2 * CHUNKS, tail, 0)

    def place(zz, carry):
        zd = (z + NZ - zz) % NZ
        for e in range(2):
            parts = []
            for yy in range(NY):
                yd = (y + NY - yy) % NY
                parts.append(terms[e, pl.ds(pl.multiple_of((yd * NZ + zd) * TOK, TOK), TOK)])
            tb[e, zz] = jnp.concatenate(parts, axis=0).astype(BF16)
        return carry

    lax.fori_loop(0, NZ, place, 0)
    ZX = NZ // NX

    def rx(dx, e):
        to = (x + dx) % NX
        return rc(tb.at[e, pl.ds(to * ZX, ZX)], tr.at[e, dx], rx_s.at[e, dx], rx_r.at[e, dx], dev(dx, 0, 0, e))

    for dx in range(1, NX):
        for e in range(2):
            rx(dx, e).start()
    rx(0, 1).start()
    sums = [tb[0, pl.ds(x * ZX, ZX)].astype(F32), None]
    rx(0, 1).wait_recv()
    sums[1] = tr[1, 0].astype(F32)
    for dx in range(1, NX):
        for e in range(2):
            rx(dx, e).wait_recv()
            sums[e] = sums[e] + tr[e, dx].astype(F32)
    low = jnp.where(c == 0, sums[0], sums[1]).reshape(ZX * NY, 1, TOK, COLS)
    high = jnp.where(c == 0, sums[1], sums[0]).reshape(ZX * NY, 1, TOK, COLS)
    out_ref[...] = jnp.concatenate([low, high], axis=1).reshape(ZX * NY * 2 * TOK, COLS).astype(BF16)

    csp.wait_send()
    ck.wait_send()
    cv.wait_send()
    cw.wait_send()

    def drain(ci, carry):
        for d in range(1, NZ):
            qz(ci, d).wait_send()
            nzc(ci, d).wait_send()
            az(ci, d).wait_send()
        for d in range(1, NY):
            qy(ci, d).wait_send()
            ny(ci, d).wait_send()
            ns(ci, d).wait_send()
            ay(ci, d).wait_send()
        return carry

    lax.fori_loop(0, CHUNKS, drain, 0)
    rx(0, 1).wait_send()
    for dx in range(1, NX):
        for e in range(2):
            rx(dx, e).wait_send()


def device_step(queries, span_keys, span_values, cache_keys, stored_values, cache_lengths, span_start, out_weight):
    vm = pl.BlockSpec(memory_space=pltpu.VMEM)
    sm = pl.BlockSpec(memory_space=pltpu.SMEM)
    hbm = pl.BlockSpec(memory_space=pltpu.HBM)
    dma = pltpu.SemaphoreType.DMA
    rows = 16
    scratch = [
        pltpu.VMEM((TOK, 16 * HD), BF16),
        pltpu.VMEM((TOK, HD), BF16),
        pltpu.VMEM((TOK, HD), BF16),
        pltpu.VMEM((SHARD, HD), BF16),
        pltpu.VMEM((SHARD, HD), BF16),
        pltpu.VMEM((2, 16, HD), BF16),
        pltpu.VMEM((KEYS, HD), BF16),
        pltpu.VMEM((KEYS, 2 * HD), BF16),
        pltpu.VMEM((2, 16 * HD, COLS), BF16),
        pltpu.VMEM((CHUNKS, NY, NZ, rows, L), BF16),
        pltpu.VMEM((CHUNKS, NY, NZ, rows, L), BF16),
        pltpu.VMEM((CHUNKS, NY, TOK, HD), F32),
        pltpu.VMEM((CHUNKS, NY, NZ, rows, L), BF16),
        pltpu.VMEM((CHUNKS, NY, TOK, HD), F32),
        pltpu.VMEM((CHUNKS, NZ, rows, L + HD), BF16),
        pltpu.VMEM((CHUNKS, NZ, rows, L + HD), BF16),
        pltpu.VMEM((CHUNKS, NY, NZ, rows, L), BF16),
        pltpu.VMEM((2, NY * NZ * TOK, COLS), F32),
        pltpu.VMEM((2, NZ, NY * TOK, COLS), BF16),
        pltpu.VMEM((2, NX, NZ // NX, NY * TOK, COLS), BF16),
        dma((8,)),
        dma((4,)),
        dma((4,)),
        dma((CHUNKS, NZ)),
        dma((CHUNKS, NZ)),
        dma((CHUNKS, NY)),
        dma((CHUNKS, NY)),
        dma((CHUNKS, NY)),
        dma((CHUNKS, NY)),
        dma((CHUNKS, NY)),
        dma((CHUNKS, NY)),
        dma((CHUNKS, NZ)),
        dma((CHUNKS, NZ)),
        dma((CHUNKS, NZ)),
        dma((CHUNKS, NZ)),
        dma((CHUNKS, NY)),
        dma((CHUNKS, NY)),
        dma((2, NX)),
        dma((2, NX)),
    ]
    return pl.pallas_call(
        kernel,
        out_shape=jax.ShapeDtypeStruct((NZ // NX * NY * 2 * TOK, COLS), BF16),
        in_specs=[hbm, hbm, hbm, sm, sm, hbm, hbm, hbm],
        out_specs=vm,
        scratch_shapes=scratch,
        compiler_params=pltpu.CompilerParams(
            collective_id=0, has_side_effects=True, vmem_limit_bytes=60 << 20
        ),
    )(queries, span_keys, span_values, cache_lengths, span_start, cache_keys, stored_values, out_weight)


def solution(mesh):
    return jax.shard_map(
        device_step,
        mesh=mesh,
        in_specs=(
            P("ctx", "tp"),
            P("ctx", "tp"),
            P("ctx", "tp"),
            P("ctx", "tp"),
            P("ctx", "tp"),
            P("ctx"),
            P(),
            P("tp", "ctx"),
        ),
        out_specs=P("tp", "ctx"),
        check_vma=False,
    )
```

```python
import functools
import math

import jax
import jax.numpy as jnp
from jax import lax
from jax.experimental import pallas as pl
from jax.experimental.pallas import tpu as pltpu
from jax.sharding import PartitionSpec as P

MESH = pl.DeviceIdType.MESH
F32, BF16 = jnp.float32, jnp.bfloat16
NX, NY, NZ, CORES = 4, 4, 8, 2
HD = 128
TOK = 8
SHARD = 1024
CHUNKS = 4
HL = 8 // CHUNKS
L = HL * HD
SPAN_PAD = 128
KEYS = CORES * SHARD + SPAN_PAD
COLS = 256
DEAD = -1e30
SCALE = math.log2(math.e) / math.sqrt(HD)
Y_ORDER = (1, 3, 2)
KB = 512


def nt(a, b):
    return lax.dot_general(a, b, (((1,), (1,)), ((), ())), preferred_element_type=F32)


def nn(a, b):
    return jnp.dot(a, b, preferred_element_type=F32)


def kernel(
    q_ref, sk_ref, sv_ref, len_ref, start_ref, ck_ref, cv_ref, w_ref, out_ref,
    qraw, skraw, svraw, kraw, vraw, span, keys, vals, weight, qg, ob, st, on, sn, nz, nr, ag, terms, tb, tr,
    loc, bar_s, bar_r, qz_s, qz_r, qd_s, qd_r, qy_s, qy_r, ny_s, ny_r, ns_s, ns_r, nz_s, nz_r,
    az_s, az_r, ay_s, ay_r, rx_s, rx_r,
):
    ctx = lax.axis_index("ctx")
    x = lax.axis_index("tp")
    c = ctx % 2
    y = (ctx // 2) % NY
    z = ctx // (2 * NY)
    chip = z * NY + y

    def dev(dx, dy, dz, dc):
        return ((((z + dz % NZ) % NZ) * NY + (y + dy % NY) % NY) * 2 + (c + dc) % 2, (x + dx % NX) % NX)

    def rc(src, dst, ss, rs, to):
        return pltpu.make_async_remote_copy(
            src_ref=src, dst_ref=dst, send_sem=ss, recv_sem=rs, device_id=to, device_id_type=MESH
        )

    lk = pltpu.make_async_copy(ck_ref, kraw, loc.at[0])
    lv = pltpu.make_async_copy(cv_ref, vraw, loc.at[1])
    lw = pltpu.make_async_copy(w_ref, weight.at[0], loc.at[2])
    small = [
        pltpu.make_async_copy(a, b, loc.at[3 + i])
        for i, (a, b) in enumerate(
            ((q_ref, qraw), (sk_ref, skraw), (sv_ref, svraw))
        )
    ]
    for cp in small:
        cp.start()
    lk.start()
    lv.start()
    lw.start()

    peers = [dev(0, 0, 0, 1)]
    peers += [dev(0, d, 0, 0) for d in range(1, NY)]
    peers += [dev(0, 0, d, 0) for d in range(1, NZ)]
    peers += [dev(d, 0, 0, e) for d in range(1, NX) for e in range(2)]
    barrier = pltpu.get_barrier_semaphore()
    for p in peers:
        pl.semaphore_signal(barrier, inc=1, device_id=p, device_id_type=MESH)

    for cp in small:
        cp.wait()
    qf = qraw[...].astype(F32)
    qf = jnp.concatenate([qf[:, : 8 * HD], qf[:, 8 * HD :]], axis=0).astype(BF16)
    for ci in range(CHUNKS):
        qg[ci, 0, 0] = qf[:, ci * L : (ci + 1) * L]
    span[0] = jnp.concatenate([skraw[...].astype(F32), svraw[...].astype(F32)], axis=0).astype(BF16)

    def qz(ci, d):
        return rc(qg.at[ci, 0, 0], qg.at[ci, 0, d], qz_s.at[ci, d], qz_r.at[ci, d], dev(0, 0, d, 0))

    def qy(ci, d):
        far_z = pl.ds(1, NZ - 1)
        return rc(qg.at[ci, 0, far_z], qg.at[ci, d, far_z], qy_s.at[ci, d], qy_r.at[ci, d], dev(0, d, 0, 0))

    def qd(ci, d, k):
        e = (0, 1, NZ - 1)[k]
        return rc(qg.at[ci, 0, 0], qg.at[ci, d, e], qd_s.at[ci, d, k], qd_r.at[ci, d, k], dev(0, d, e, 0))

    def qy1(d):
        return rc(qg.at[CHUNKS - 1, 0, 0], qg.at[CHUNKS - 1, d, 0], qy_s.at[CHUNKS - 1, d], qy_r.at[CHUNKS - 1, d], dev(0, d, 0, 0))

    def qz1(d):
        return rc(
            qg.at[CHUNKS - 1, :, 0], qg.at[CHUNKS - 1, :, d], qz_s.at[CHUNKS - 1, d], qz_r.at[CHUNKS - 1, d], dev(0, 0, d, 0)
        )

    sib = dev(0, 0, 0, 1)
    own_rows = pl.ds(pl.multiple_of(c * SHARD, SHARD), SHARD)
    csp = rc(span.at[0], span.at[1], bar_s.at[0], bar_r.at[0], sib)
    ck = rc(keys.at[own_rows], keys.at[own_rows], bar_s.at[1], bar_r.at[1], sib)
    cv = rc(vals.at[own_rows], vals.at[own_rows], bar_s.at[2], bar_r.at[2], sib)
    cw = rc(weight.at[0], weight.at[1], bar_s.at[3], bar_r.at[3], sib)
    pl.semaphore_wait(barrier, len(peers))
    last = CHUNKS - 1
    for d in Y_ORDER:
        qy1(d).start()
    for ci in range(last):
        for d in (4, 3, 5, 2, 6, 1, 7):
            qz(ci, d).start()
        for d in Y_ORDER:
            for k in range(1):
                qd(ci, d, k).start()
    csp.start()
    begin = start_ref[0]
    row = lax.broadcasted_iota(jnp.int32, (SHARD, HD), 0)
    live = row < jnp.minimum(len_ref[0], begin - ctx * SHARD)
    lk.wait()
    kr = kraw[...]
    keys[own_rows] = jnp.where(live, kr.astype(F32), kr[0:1].astype(F32)).astype(BF16)
    ck.start()
    lv.wait()
    vals[own_rows, 0:HD] = jnp.where(live, vraw[...].astype(F32), 0.0).astype(BF16)
    vals[own_rows, HD:] = jnp.where(live, 1.0, 0.0).astype(BF16)
    cv.start()
    lw.wait()
    cw.start()
    csp.wait_recv()
    s_own = span[0].astype(F32)
    s_sib = span[1].astype(F32)
    first = jnp.where(c == 0, s_own, s_sib)
    second = jnp.where(c == 0, s_sib, s_own)
    base = CORES * SHARD
    keys[base : base + 16] = jnp.concatenate([first[0:8], second[0:8]], axis=0).astype(BF16)
    keys[base + 16 : KEYS] = jnp.zeros((SPAN_PAD - 16, HD), BF16)
    vals[base : base + 16, 0:HD] = jnp.concatenate([first[8:16], second[8:16]], axis=0).astype(BF16)
    vals[base : base + 16, HD:] = jnp.ones((16, HD), BF16)
    vals[base + 16 : KEYS] = jnp.zeros((SPAN_PAD - 16, 2 * HD), BF16)

    even_live = chip * (2 * SHARD) < begin
    odd_live = chip * (2 * SHARD) + SHARD < begin
    c0 = jnp.where(even_live, SCALE, 0.0).astype(F32)
    b0 = jnp.where(even_live, 0.0, DEAD).astype(F32)
    c1 = jnp.where(odd_live, SCALE, 0.0).astype(F32)
    b1 = jnp.where(odd_live, 0.0, DEAD).astype(F32)
    lane8 = lax.broadcasted_iota(jnp.int32, (TOK, HD), 1)
    lane16 = lax.broadcasted_iota(jnp.int32, (2 * TOK, HD), 1)

    def ny(ci, d):
        return rc(ob.at[ci, d], on.at[ci, d], ny_s.at[ci, d], ny_r.at[ci, d], dev(0, -d, 0, 0))

    def ns(ci, d):
        return rc(st.at[ci, d], sn.at[ci, d], ns_s.at[ci, d], ns_r.at[ci, d], dev(0, -d, 0, 0))

    def attend(pairs):
        m_rows = len(pairs) * HL * HD
        rows_i = lax.broadcasted_iota(jnp.int32, (HD, SPAN_PAD), 0)
        cols_i = lax.broadcasted_iota(jnp.int32, (HD, SPAN_PAD), 1)
        owner_z = (z + NZ - (rows_i >> 4)) & (NZ - 1)
        blocks, masks = [], []
        for ci, yd in pairs:
            qa = qg[ci, yd]
            token = (owner_z * NY + ((y + NY - yd) & (NY - 1))) * 16 + c * 8 + (rows_i & 7)
            see = (cols_i < 16) & (chip * 16 + cols_i <= token)
            for i in range(HL):
                blocks.append(qa[:, :, i * HD : (i + 1) * HD].reshape(HD, HD))
                masks.append(jnp.where(see, 0.0, 2 * DEAD))
        q2 = jnp.concatenate(blocks, axis=0)
        ss = nt(q2, keys[base:KEYS]) * SCALE + jnp.concatenate(masks, axis=0)
        m = jnp.maximum(jnp.broadcast_to(jnp.max(ss, axis=1, keepdims=True), (m_rows, HD)), DEAD)
        acc = nn(jnp.exp2(ss - m).astype(BF16), vals[base:KEYS])
        for kb in range(0, CORES * SHARD, KB):
            cs, bs = (c0, b0) if kb < SHARD else (c1, b1)
            s = nt(q2, keys[kb : kb + KB])
            top = functools.reduce(jnp.maximum, [s[:, j : j + HD] for j in range(0, KB, HD)])
            top = jnp.broadcast_to(jnp.max(top, axis=1, keepdims=True), (m_rows, HD)) * cs + bs
            new = jnp.maximum(m, top)
            keep = jnp.exp2(m - new)
            off = bs - new
            p = jnp.concatenate(
                [jnp.exp2(s[:, j : j + HD] * cs + off).astype(BF16) for j in range(0, KB, HD)], axis=1
            )
            acc = acc * jnp.concatenate([keep, keep], axis=1) + nn(p, vals[kb : kb + KB])
            m = new
        total = jnp.maximum(acc[:, HD:], 1e-30)
        o = (acc[:, :HD] / total).astype(BF16)
        lse = m + jnp.log2(total)
        for b, (ci, yd) in enumerate(pairs):
            tile = jnp.zeros((TOK, HD), F32)
            for i in range(HL):
                r = (b * HL + i) * HD
                ob[ci, yd, :, :, i * HD : (i + 1) * HD] = o[r : r + HD].reshape(NZ, 16, HD)
                for zd in range(NZ):
                    for hh in range(2):
                        w = r + zd * 16 + hh * 8
                        tile = jnp.where(lane8 == zd * 16 + i * 2 + hh, lse[w : w + 8], tile)
            st[ci, yd] = tile

    def nzc(ci, d):
        return rc(nz.at[ci, d], nr.at[ci, d], nz_s.at[ci, d], nz_r.at[ci, d], dev(0, 0, -d, 0))

    def az(ci, d):
        return rc(ag.at[ci, 0, 0], ag.at[ci, 0, d], az_s.at[ci, d], az_r.at[ci, d], dev(0, 0, d, 0))

    def ay(ci, d):
        return rc(ag.at[ci, 0], ag.at[ci, d], ay_s.at[ci, d], ay_r.at[ci, d], dev(0, d, 0, 0))

    def merge(parts):
        top = functools.reduce(jnp.maximum, [lse for lse, _ in parts])
        ws = [jnp.exp2(lse - top) for lse, _ in parts]
        total = functools.reduce(jnp.add, ws)
        num = functools.reduce(jnp.add, [w * o.astype(F32) for w, (_, o) in zip(ws, parts)])
        return num / total, top + jnp.log2(total)

    def reduce_y(ci):
        for d in range(1, NY):
            ny(ci, d).wait_recv()
            ns(ci, d).wait_recv()
        tiles = [st[ci, 0]] + [sn[ci, d] for d in range(1, NY)]
        for zd in range(NZ):
            stat = jnp.zeros((16, HD), F32)
            for i in range(HL):
                parts = []
                for d in range(NY):
                    k = zd * 16 + i * 2
                    lse = jnp.concatenate(
                        [jnp.broadcast_to(tiles[d][:, k + hh : k + hh + 1], (8, HD)) for hh in range(2)], axis=0
                    )
                    src = ob if d == 0 else on
                    parts.append((lse, src[ci, d, zd, :, i * HD : (i + 1) * HD]))
                o, lse = merge(parts)
                nz[ci, zd, :, i * HD : (i + 1) * HD] = o.astype(BF16)
                hi = lse.astype(BF16).astype(F32)
                mid = (lse - hi).astype(BF16).astype(F32)
                lo = lse - hi - mid
                for p, v in enumerate((hi, mid, lo)):
                    stat = jnp.where(lane16 == i * 4 + p, v, stat)
            nz[ci, zd, :, L:] = stat.astype(BF16)
        for d in (4, 3, 5, 2, 6, 1, 7):
            nzc(ci, d).start()

    def reduce_z(ci):
        for d in range(1, NZ):
            nzc(ci, d).wait_recv()
        for i in range(HL):
            parts = []
            for d in range(NZ):
                src = nz if d == 0 else nr
                stat = src[ci, d, :, L:].astype(F32)
                pick = (lane16 >= i * 4) & (lane16 < i * 4 + 3)
                lse = jnp.broadcast_to(jnp.sum(jnp.where(pick, stat, 0.0), axis=1, keepdims=True), (16, HD))
                parts.append((lse, src[ci, d, :, i * HD : (i + 1) * HD]))
            o, _ = merge(parts)
            ag[ci, 0, 0, :, i * HD : (i + 1) * HD] = o.astype(BF16)
        for d in (4, 3, 5, 2, 6, 1, 7):
            az(ci, d).start()

    def spread_y(ci):
        for d in range(1, NZ):
            az(ci, d).wait_recv()
        for d in Y_ORDER:
            ay(ci, d).start()

    terms[...] = jnp.zeros_like(terms)

    def project(ci, sides):
        a = ag[ci].astype(F32).reshape(NY * NZ, 16, L)
        for hh in range(2):
            ah = a[:, hh * 8 : (hh + 1) * 8].reshape(NY * NZ * TOK, L).astype(BF16)
            rows = pl.ds(pl.multiple_of(hh * 8 * HD + ci * L, L), L)
            for e in sides:
                terms[e] += nn(ah, weight[e, rows])

    def wait_ay(ci):
        for d in range(1, NY):
            ay(ci, d).wait_recv()

    def send_y(ci, d):
        ny(ci, d).start()
        ns(ci, d).start()

    def early(t, carry):
        @pl.when(t == 0)
        def _():
            for ci in range(last):
                for d in range(1, NZ):
                    qz(ci, d).wait_recv()
                for d in Y_ORDER:
                    qy(ci, d).start()
                if ci == 0:
                    for d in Y_ORDER:
                        qy1(d).wait_recv()
                    for d in range(1, NZ):
                        qz1(d).start()
            ck.wait_recv()
            cv.wait_recv()

        @pl.when(t > 0)
        def _():
            for d in Y_ORDER:
                qy(t - 1, d).wait_recv()
                for k in range(1):
                    qd(t - 1, d, k).wait_recv()

        at0 = t == 0
        attend([(jnp.where(at0, i, t - 1), jnp.where(at0, 0, d)) for i, d in enumerate((2, 1, 3))])

        @pl.when(t > 0)
        def _():
            for d in (2, 1, 3):
                send_y(t - 1, d)

        @pl.when(t == CHUNKS - 1)
        def _():
            reduce_y(0)

        return carry

    lax.fori_loop(0, CHUNKS, early, 0)
    for d in range(1, NZ):
        qz1(d).wait_recv()

    def late(t, carry):
        attend([(last, jnp.where(t == 0, a, b)) for a, b in ((2, 3), (1, 0))])

        @pl.when(t == 0)
        def _():
            send_y(last, 2)
            send_y(last, 1)
            reduce_y(1)

        @pl.when(t == 1)
        def _():
            send_y(last, 3)

        return carry

    lax.fori_loop(0, 2, late, 0)
    cw.wait_recv()

    def tail(u, carry):
        @pl.when(u < CHUNKS)
        def _():
            reduce_z(u)

        @pl.when(u < 2)
        def _():
            reduce_y(u + 2)

        @pl.when(u >= 1)
        def _():
            spread_y(u - 1)

        return carry

    lax.fori_loop(0, CHUNKS + 1, tail, 0)

    def drain(ci, carry):
        for d in range(1, NZ):
            qz(ci, d).wait_send()
            nzc(ci, d).wait_send()
            az(ci, d).wait_send()
        for d in range(1, NY):
            qy(ci, d).wait_send()
            for k in range(1):
                qd(ci, d, k).wait_send()
            ny(ci, d).wait_send()
            ns(ci, d).wait_send()
        wait_ay(ci)
        project(ci, (0, 1))
        return carry

    lax.fori_loop(0, last, drain, 0)
    for d in range(1, NZ):
        qz1(d).wait_send()
        nzc(last, d).wait_send()
        az(last, d).wait_send()
    for d in range(1, NY):
        qy1(d).wait_send()
        ny(last, d).wait_send()
        ns(last, d).wait_send()
    csp.wait_send()
    ck.wait_send()
    cv.wait_send()
    cw.wait_send()
    wait_ay(last)

    ZX = NZ // NX

    def rx(dx, e):
        to = (x + dx) % NX
        return rc(tb.at[e, pl.ds(to * ZX, ZX)], tr.at[e, dx], rx_s.at[e, dx], rx_r.at[e, dx], dev(dx, 0, 0, e))

    for e in (1, 0):
        project(last, (e,))

        def place(zz, carry):
            zd = (z + NZ - zz) % NZ
            parts = []
            for yy in range(NY):
                yd = (y + NY - yy) % NY
                parts.append(terms[e, pl.ds(pl.multiple_of((yd * NZ + zd) * TOK, TOK), TOK)])
            tb[e, zz] = jnp.concatenate(parts, axis=0).astype(BF16)
            return carry

        lax.fori_loop(0, NZ, place, 0)
        for dx in (2, 1, 3):
            rx(dx, e).start()
        if e == 1:
            rx(0, 1).start()
    sums = [tb[0, pl.ds(x * ZX, ZX)].astype(F32), None]
    rx(0, 1).wait_recv()
    sums[1] = tr[1, 0].astype(F32)
    for e in (1, 0):
        for dx in range(1, NX):
            rx(dx, e).wait_recv()
            sums[e] = sums[e] + tr[e, dx].astype(F32)
    low = jnp.where(c == 0, sums[0], sums[1]).reshape(ZX * NY, 1, TOK, COLS)
    high = jnp.where(c == 0, sums[1], sums[0]).reshape(ZX * NY, 1, TOK, COLS)
    out_ref[...] = jnp.concatenate([low, high], axis=1).reshape(ZX * NY * 2 * TOK, COLS).astype(BF16)

    for ci in range(CHUNKS):
        for d in range(1, NY):
            ay(ci, d).wait_send()
    rx(0, 1).wait_send()
    for dx in range(1, NX):
        for e in range(2):
            rx(dx, e).wait_send()


def device_step(queries, span_keys, span_values, cache_keys, stored_values, cache_lengths, span_start, out_weight):
    vm = pl.BlockSpec(memory_space=pltpu.VMEM)
    sm = pl.BlockSpec(memory_space=pltpu.SMEM)
    hbm = pl.BlockSpec(memory_space=pltpu.HBM)
    dma = pltpu.SemaphoreType.DMA
    rows = 16
    scratch = [
        pltpu.VMEM((TOK, 16 * HD), BF16),
        pltpu.VMEM((TOK, HD), BF16),
        pltpu.VMEM((TOK, HD), BF16),
        pltpu.VMEM((SHARD, HD), BF16),
        pltpu.VMEM((SHARD, HD), BF16),
        pltpu.VMEM((2, 16, HD), BF16),
        pltpu.VMEM((KEYS, HD), BF16),
        pltpu.VMEM((KEYS, 2 * HD), BF16),
        pltpu.VMEM((2, 16 * HD, COLS), BF16),
        pltpu.VMEM((CHUNKS, NY, NZ, rows, L), BF16),
        pltpu.VMEM((CHUNKS, NY, NZ, rows, L), BF16),
        pltpu.VMEM((CHUNKS, NY, TOK, HD), F32),
        pltpu.VMEM((CHUNKS, NY, NZ, rows, L), BF16),
        pltpu.VMEM((CHUNKS, NY, TOK, HD), F32),
        pltpu.VMEM((CHUNKS, NZ, rows, L + HD), BF16),
        pltpu.VMEM((CHUNKS, NZ, rows, L + HD), BF16),
        pltpu.VMEM((CHUNKS, NY, NZ, rows, L), BF16),
        pltpu.VMEM((2, NY * NZ * TOK, COLS), F32),
        pltpu.VMEM((2, NZ, NY * TOK, COLS), BF16),
        pltpu.VMEM((2, NX, NZ // NX, NY * TOK, COLS), BF16),
        dma((8,)),
        dma((4,)),
        dma((4,)),
        dma((CHUNKS, NZ)),
        dma((CHUNKS, NZ)),
        dma((CHUNKS, NY, 1)),
        dma((CHUNKS, NY, 1)),
        dma((CHUNKS, NY)),
        dma((CHUNKS, NY)),
        dma((CHUNKS, NY)),
        dma((CHUNKS, NY)),
        dma((CHUNKS, NY)),
        dma((CHUNKS, NY)),
        dma((CHUNKS, NZ)),
        dma((CHUNKS, NZ)),
        dma((CHUNKS, NZ)),
        dma((CHUNKS, NZ)),
        dma((CHUNKS, NY)),
        dma((CHUNKS, NY)),
        dma((2, NX)),
        dma((2, NX)),
    ]
    return pl.pallas_call(
        kernel,
        out_shape=jax.ShapeDtypeStruct((NZ // NX * NY * 2 * TOK, COLS), BF16),
        in_specs=[hbm, hbm, hbm, sm, sm, hbm, hbm, hbm],
        out_specs=vm,
        scratch_shapes=scratch,
        compiler_params=pltpu.CompilerParams(
            collective_id=0, has_side_effects=True, vmem_limit_bytes=60 << 20
        ),
    )(queries, span_keys, span_values, cache_lengths, span_start, cache_keys, stored_values, out_weight)


def solution(mesh):
    return jax.shard_map(
        device_step,
        mesh=mesh,
        in_specs=(
            P("ctx", "tp"),
            P("ctx", "tp"),
            P("ctx", "tp"),
            P("ctx", "tp"),
            P("ctx", "tp"),
            P("ctx"),
            P(),
            P("tp", "ctx"),
        ),
        out_specs=P("tp", "ctx"),
        check_vma=False,
    )
```

```python
import functools
import math

import jax
import jax.numpy as jnp
from jax import lax
from jax.experimental import pallas as pl
from jax.experimental.pallas import tpu as pltpu
from jax.sharding import PartitionSpec as P

MESH = pl.DeviceIdType.MESH
F32, BF16 = jnp.float32, jnp.bfloat16
NX, NY, NZ, CORES = 4, 4, 8, 2
HD = 128
TOK = 8
SHARD = 1024
CHUNKS = 4
HL = 8 // CHUNKS
L = HL * HD
SPAN_PAD = 128
KEYS = CORES * SHARD + SPAN_PAD
COLS = 256
DEAD = -1e30
SCALE = math.log2(math.e) / math.sqrt(HD)
Y_ORDER = (1, 3, 2)
KB = 512


def nt(a, b):
    return lax.dot_general(a, b, (((1,), (1,)), ((), ())), preferred_element_type=F32)


def nn(a, b):
    return jnp.dot(a, b, preferred_element_type=F32)


def kernel(
    q_ref, sk_ref, sv_ref, len_ref, start_ref, ck_ref, cv_ref, w_ref, out_ref,
    qraw, skraw, svraw, kraw, vraw, span, keys, vals, weight, qg, ob, st, on, sn, nz, nr, ag, terms, tb, tr,
    loc, bar_s, bar_r, qz_s, qz_r, qd_s, qd_r, qy_s, qy_r, ny_s, ny_r, ns_s, ns_r, nz_s, nz_r,
    az_s, az_r, ay_s, ay_r, rx_s, rx_r,
):
    ctx = lax.axis_index("ctx")
    x = lax.axis_index("tp")
    c = ctx % 2
    y = (ctx // 2) % NY
    z = ctx // (2 * NY)
    chip = z * NY + y

    def dev(dx, dy, dz, dc):
        return ((((z + dz % NZ) % NZ) * NY + (y + dy % NY) % NY) * 2 + (c + dc) % 2, (x + dx % NX) % NX)

    def rc(src, dst, ss, rs, to):
        return pltpu.make_async_remote_copy(
            src_ref=src, dst_ref=dst, send_sem=ss, recv_sem=rs, device_id=to, device_id_type=MESH
        )

    peers = [dev(0, 0, 0, 1)]
    peers += [dev(0, d, 0, 0) for d in range(1, NY)]
    peers += [dev(0, 0, d, 0) for d in (4, 3, 5, 2, 6, 1, 7)]
    peers += [dev(d, 0, 0, e) for d in range(1, NX) for e in range(2)]
    barrier = pltpu.get_barrier_semaphore()
    for p in peers:
        pl.semaphore_signal(barrier, inc=1, device_id=p, device_id_type=MESH)

    lk = pltpu.make_async_copy(ck_ref, kraw, loc.at[0])
    lv = pltpu.make_async_copy(cv_ref, vraw, loc.at[1])
    lw = pltpu.make_async_copy(w_ref, weight.at[0], loc.at[2])
    small = [
        pltpu.make_async_copy(a, b, loc.at[3 + i])
        for i, (a, b) in enumerate(
            ((q_ref, qraw), (sk_ref, skraw), (sv_ref, svraw))
        )
    ]
    for cp in small:
        cp.start()
    lk.start()
    lv.start()
    lw.start()

    for cp in small:
        cp.wait()
    qf = qraw[...].astype(F32)
    qf = jnp.concatenate([qf[:, : 8 * HD], qf[:, 8 * HD :]], axis=0).astype(BF16)
    for ci in range(CHUNKS):
        qg[ci, 0, 0] = qf[:, ci * L : (ci + 1) * L]
    span[0] = jnp.concatenate([skraw[...].astype(F32), svraw[...].astype(F32)], axis=0).astype(BF16)

    def qz(ci, d):
        return rc(qg.at[ci, 0, 0], qg.at[ci, 0, d], qz_s.at[ci, d], qz_r.at[ci, d], dev(0, 0, d, 0))

    def qy(ci, d):
        far_z = pl.ds(1, NZ - 1)
        return rc(qg.at[ci, 0, far_z], qg.at[ci, d, far_z], qy_s.at[ci, d], qy_r.at[ci, d], dev(0, d, 0, 0))

    def qd(ci, d, k):
        e = (0, 1, NZ - 1)[k]
        return rc(qg.at[ci, 0, 0], qg.at[ci, d, e], qd_s.at[ci, d, k], qd_r.at[ci, d, k], dev(0, d, e, 0))

    def qy1(d):
        return rc(qg.at[CHUNKS - 1, 0, 0], qg.at[CHUNKS - 1, d, 0], qy_s.at[CHUNKS - 1, d], qy_r.at[CHUNKS - 1, d], dev(0, d, 0, 0))

    def qz1(d):
        return rc(
            qg.at[CHUNKS - 1, :, 0], qg.at[CHUNKS - 1, :, d], qz_s.at[CHUNKS - 1, d], qz_r.at[CHUNKS - 1, d], dev(0, 0, d, 0)
        )

    sib = dev(0, 0, 0, 1)
    own_rows = pl.ds(pl.multiple_of(c * SHARD, SHARD), SHARD)
    csp = rc(span.at[0], span.at[1], bar_s.at[0], bar_r.at[0], sib)
    ck = rc(keys.at[own_rows], keys.at[own_rows], bar_s.at[1], bar_r.at[1], sib)
    cv = rc(vals.at[own_rows], vals.at[own_rows], bar_s.at[2], bar_r.at[2], sib)
    cw = rc(weight.at[0], weight.at[1], bar_s.at[3], bar_r.at[3], sib)
    pl.semaphore_wait(barrier, len(peers))
    last = CHUNKS - 1
    for d in Y_ORDER:
        qy1(d).start()
    for ci in range(last):
        for d in (4, 3, 5, 2, 6, 1, 7):
            qz(ci, d).start()
        for d in Y_ORDER:
            for k in range(1):
                qd(ci, d, k).start()
    csp.start()
    begin = start_ref[0]
    row = lax.broadcasted_iota(jnp.int32, (SHARD, HD), 0)
    live = row < jnp.minimum(len_ref[0], begin - ctx * SHARD)
    lk.wait()
    kr = kraw[...]
    keys[own_rows] = jnp.where(live, kr.astype(F32), kr[0:1].astype(F32)).astype(BF16)
    ck.start()
    lv.wait()
    vals[own_rows, 0:HD] = jnp.where(live, vraw[...].astype(F32), 0.0).astype(BF16)
    vals[own_rows, HD:] = jnp.where(live, 1.0, 0.0).astype(BF16)
    cv.start()
    lw.wait()
    cw.start()
    csp.wait_recv()
    s_own = span[0].astype(F32)
    s_sib = span[1].astype(F32)
    first = jnp.where(c == 0, s_own, s_sib)
    second = jnp.where(c == 0, s_sib, s_own)
    base = CORES * SHARD
    keys[base : base + 16] = jnp.concatenate([first[0:8], second[0:8]], axis=0).astype(BF16)
    keys[base + 16 : KEYS] = jnp.zeros((SPAN_PAD - 16, HD), BF16)
    vals[base : base + 16, 0:HD] = jnp.concatenate([first[8:16], second[8:16]], axis=0).astype(BF16)
    vals[base : base + 16, HD:] = jnp.ones((16, HD), BF16)
    vals[base + 16 : KEYS] = jnp.zeros((SPAN_PAD - 16, 2 * HD), BF16)

    even_live = chip * (2 * SHARD) < begin
    odd_live = chip * (2 * SHARD) + SHARD < begin
    c0 = jnp.where(even_live, SCALE, 0.0).astype(F32)
    b0 = jnp.where(even_live, 0.0, DEAD).astype(F32)
    c1 = jnp.where(odd_live, SCALE, 0.0).astype(F32)
    b1 = jnp.where(odd_live, 0.0, DEAD).astype(F32)
    lane8 = lax.broadcasted_iota(jnp.int32, (TOK, HD), 1)
    lane16 = lax.broadcasted_iota(jnp.int32, (2 * TOK, HD), 1)

    def ny(ci, d):
        return rc(ob.at[ci, d], on.at[ci, d], ny_s.at[ci, d], ny_r.at[ci, d], dev(0, -d, 0, 0))

    def ns(ci, d):
        return rc(st.at[ci, d], sn.at[ci, d], ns_s.at[ci, d], ns_r.at[ci, d], dev(0, -d, 0, 0))

    def attend(pairs):
        m_rows = len(pairs) * HL * HD
        rows_i = lax.broadcasted_iota(jnp.int32, (HD, SPAN_PAD), 0)
        cols_i = lax.broadcasted_iota(jnp.int32, (HD, SPAN_PAD), 1)
        owner_z = (z + NZ - (rows_i >> 4)) & (NZ - 1)
        blocks, masks = [], []
        for ci, yd in pairs:
            qa = qg[ci, yd]
            token = (owner_z * NY + ((y + NY - yd) & (NY - 1))) * 16 + c * 8 + (rows_i & 7)
            see = (cols_i < 16) & (chip * 16 + cols_i <= token)
            for i in range(HL):
                blocks.append(qa[:, :, i * HD : (i + 1) * HD].reshape(HD, HD))
                masks.append(jnp.where(see, 0.0, 2 * DEAD))
        q2 = jnp.concatenate(blocks, axis=0)
        ss = nt(q2, keys[base:KEYS]) * SCALE + jnp.concatenate(masks, axis=0)
        m = jnp.maximum(jnp.broadcast_to(jnp.max(ss, axis=1, keepdims=True), (m_rows, HD)), DEAD)
        acc = nn(jnp.exp2(ss - m).astype(BF16), vals[base:KEYS])
        for kb in range(0, CORES * SHARD, KB):
            cs, bs = (c0, b0) if kb < SHARD else (c1, b1)
            s = nt(q2, keys[kb : kb + KB])
            top = functools.reduce(jnp.maximum, [s[:, j : j + HD] for j in range(0, KB, HD)])
            top = jnp.broadcast_to(jnp.max(top, axis=1, keepdims=True), (m_rows, HD)) * cs + bs
            new = jnp.maximum(m, top)
            keep = jnp.exp2(m - new)
            off = bs - new
            p = jnp.concatenate(
                [jnp.exp2(s[:, j : j + HD] * cs + off).astype(BF16) for j in range(0, KB, HD)], axis=1
            )
            acc = acc * jnp.concatenate([keep, keep], axis=1) + nn(p, vals[kb : kb + KB])
            m = new
        total = jnp.maximum(acc[:, HD:], 1e-30)
        o = (acc[:, :HD] / total).astype(BF16)
        lse = m + jnp.log2(total)
        for b, (ci, yd) in enumerate(pairs):
            tile = jnp.zeros((TOK, HD), F32)
            for i in range(HL):
                r = (b * HL + i) * HD
                ob[ci, yd, :, :, i * HD : (i + 1) * HD] = o[r : r + HD].reshape(NZ, 16, HD)
                for zd in range(NZ):
                    for hh in range(2):
                        w = r + zd * 16 + hh * 8
                        tile = jnp.where(lane8 == zd * 16 + i * 2 + hh, lse[w : w + 8], tile)
            st[ci, yd] = tile

    def nzc(ci, d):
        return rc(nz.at[ci, d], nr.at[ci, d], nz_s.at[ci, d], nz_r.at[ci, d], dev(0, 0, -d, 0))

    def az(ci, d):
        return rc(ag.at[ci, 0, 0], ag.at[ci, 0, d], az_s.at[ci, d], az_r.at[ci, d], dev(0, 0, d, 0))

    def ay(ci, d):
        return rc(ag.at[ci, 0], ag.at[ci, d], ay_s.at[ci, d], ay_r.at[ci, d], dev(0, d, 0, 0))

    def merge(parts):
        top = functools.reduce(jnp.maximum, [lse for lse, _ in parts])
        ws = [jnp.exp2(lse - top) for lse, _ in parts]
        total = functools.reduce(jnp.add, ws)
        num = functools.reduce(jnp.add, [w * o.astype(F32) for w, (_, o) in zip(ws, parts)])
        return num / total, top + jnp.log2(total)

    def reduce_y(ci):
        for d in range(1, NY):
            ny(ci, d).wait_recv()
            ns(ci, d).wait_recv()
        tiles = [st[ci, 0]] + [sn[ci, d] for d in range(1, NY)]
        for zd in range(NZ):
            stat = jnp.zeros((16, HD), F32)
            for i in range(HL):
                parts = []
                for d in range(NY):
                    k = zd * 16 + i * 2
                    lse = jnp.concatenate(
                        [jnp.broadcast_to(tiles[d][:, k + hh : k + hh + 1], (8, HD)) for hh in range(2)], axis=0
                    )
                    src = ob if d == 0 else on
                    parts.append((lse, src[ci, d, zd, :, i * HD : (i + 1) * HD]))
                o, lse = merge(parts)
                nz[ci, zd, :, i * HD : (i + 1) * HD] = o.astype(BF16)
                hi = lse.astype(BF16).astype(F32)
                mid = (lse - hi).astype(BF16).astype(F32)
                lo = lse - hi - mid
                for p, v in enumerate((hi, mid, lo)):
                    stat = jnp.where(lane16 == i * 4 + p, v, stat)
            nz[ci, zd, :, L:] = stat.astype(BF16)
        for d in (4, 3, 5, 2, 6, 1, 7):
            nzc(ci, d).start()

    def reduce_z(ci):
        for d in range(1, NZ):
            nzc(ci, d).wait_recv()
        for i in range(HL):
            parts = []
            for d in range(NZ):
                src = nz if d == 0 else nr
                stat = src[ci, d, :, L:].astype(F32)
                pick = (lane16 >= i * 4) & (lane16 < i * 4 + 3)
                lse = jnp.broadcast_to(jnp.sum(jnp.where(pick, stat, 0.0), axis=1, keepdims=True), (16, HD))
                parts.append((lse, src[ci, d, :, i * HD : (i + 1) * HD]))
            o, _ = merge(parts)
            ag[ci, 0, 0, :, i * HD : (i + 1) * HD] = o.astype(BF16)
        for d in (4, 3, 5, 2, 6, 1, 7):
            az(ci, d).start()

    def spread_y(ci):
        for d in range(1, NZ):
            az(ci, d).wait_recv()
        for d in Y_ORDER:
            ay(ci, d).start()

    terms[...] = jnp.zeros_like(terms)

    def project(ci, sides):
        a = ag[ci].astype(F32).reshape(NY * NZ, 16, L)
        for hh in range(2):
            ah = a[:, hh * 8 : (hh + 1) * 8].reshape(NY * NZ * TOK, L).astype(BF16)
            rows = pl.ds(pl.multiple_of(hh * 8 * HD + ci * L, L), L)
            for e in sides:
                terms[e] += nn(ah, weight[e, rows])

    def wait_ay(ci):
        for d in range(1, NY):
            ay(ci, d).wait_recv()

    def send_y(ci, d):
        ny(ci, d).start()
        ns(ci, d).start()

    def early(t, carry):
        @pl.when(t == 0)
        def _():
            for ci in range(last):
                for d in range(1, NZ):
                    qz(ci, d).wait_recv()
                for d in Y_ORDER:
                    qy(ci, d).start()
                if ci == 0:
                    for d in Y_ORDER:
                        qy1(d).wait_recv()
                    for d in (4, 3, 5, 2, 6, 1, 7):
                        qz1(d).start()
            ck.wait_recv()
            cv.wait_recv()

        @pl.when(t > 0)
        def _():
            for d in Y_ORDER:
                qy(t - 1, d).wait_recv()
                for k in range(1):
                    qd(t - 1, d, k).wait_recv()

        at0 = t == 0
        attend([(jnp.where(at0, i, t - 1), jnp.where(at0, 0, d)) for i, d in enumerate((2, 1, 3))])

        @pl.when(t > 0)
        def _():
            for d in (2, 1, 3):
                send_y(t - 1, d)

        @pl.when(t == CHUNKS - 1)
        def _():
            reduce_y(0)

        return carry

    lax.fori_loop(0, CHUNKS, early, 0)
    for d in range(1, NZ):
        qz1(d).wait_recv()

    def late(t, carry):
        attend([(last, jnp.where(t == 0, a, b)) for a, b in ((2, 3), (1, 0))])

        @pl.when(t == 0)
        def _():
            send_y(last, 2)
            send_y(last, 1)
            reduce_y(1)

        @pl.when(t == 1)
        def _():
            send_y(last, 3)

        return carry

    lax.fori_loop(0, 2, late, 0)
    cw.wait_recv()

    def tail(u, carry):
        @pl.when(u < CHUNKS)
        def _():
            reduce_z(u)

        @pl.when(u < 2)
        def _():
            reduce_y(u + 2)

        @pl.when(u >= 1)
        def _():
            spread_y(u - 1)

        return carry

    lax.fori_loop(0, CHUNKS + 1, tail, 0)

    def drain(ci, carry):
        for d in range(1, NZ):
            qz(ci, d).wait_send()
            nzc(ci, d).wait_send()
            az(ci, d).wait_send()
        for d in range(1, NY):
            qy(ci, d).wait_send()
            for k in range(1):
                qd(ci, d, k).wait_send()
            ny(ci, d).wait_send()
            ns(ci, d).wait_send()
        wait_ay(ci)
        project(ci, (0, 1))
        return carry

    lax.fori_loop(0, last, drain, 0)
    for d in range(1, NZ):
        qz1(d).wait_send()
        nzc(last, d).wait_send()
        az(last, d).wait_send()
    for d in range(1, NY):
        qy1(d).wait_send()
        ny(last, d).wait_send()
        ns(last, d).wait_send()
    csp.wait_send()
    ck.wait_send()
    cv.wait_send()
    cw.wait_send()
    wait_ay(last)

    ZX = NZ // NX

    def rx(dx, e):
        to = (x + dx) % NX
        return rc(tb.at[e, pl.ds(to * ZX, ZX)], tr.at[e, dx], rx_s.at[e, dx], rx_r.at[e, dx], dev(dx, 0, 0, e))

    for e in (1, 0):
        project(last, (e,))

        def place(zz, carry):
            zd = (z + NZ - zz) % NZ
            parts = []
            for yy in range(NY):
                yd = (y + NY - yy) % NY
                parts.append(terms[e, pl.ds(pl.multiple_of((yd * NZ + zd) * TOK, TOK), TOK)])
            tb[e, zz] = jnp.concatenate(parts, axis=0).astype(BF16)
            return carry

        lax.fori_loop(0, NZ, place, 0)
        for dx in (2, 1, 3):
            rx(dx, e).start()
        if e == 1:
            rx(0, 1).start()
    sums = [tb[0, pl.ds(x * ZX, ZX)].astype(F32), None]
    rx(0, 1).wait_recv()
    sums[1] = tr[1, 0].astype(F32)
    for e in (1, 0):
        for dx in range(1, NX):
            rx(dx, e).wait_recv()
            sums[e] = sums[e] + tr[e, dx].astype(F32)
    low = jnp.where(c == 0, sums[0], sums[1]).reshape(ZX * NY, 1, TOK, COLS)
    high = jnp.where(c == 0, sums[1], sums[0]).reshape(ZX * NY, 1, TOK, COLS)
    out_ref[...] = jnp.concatenate([low, high], axis=1).reshape(ZX * NY * 2 * TOK, COLS).astype(BF16)

    for ci in range(CHUNKS):
        for d in range(1, NY):
            ay(ci, d).wait_send()
    rx(0, 1).wait_send()
    for dx in range(1, NX):
        for e in range(2):
            rx(dx, e).wait_send()


def device_step(queries, span_keys, span_values, cache_keys, stored_values, cache_lengths, span_start, out_weight):
    vm = pl.BlockSpec(memory_space=pltpu.VMEM)
    sm = pl.BlockSpec(memory_space=pltpu.SMEM)
    hbm = pl.BlockSpec(memory_space=pltpu.HBM)
    dma = pltpu.SemaphoreType.DMA
    rows = 16
    scratch = [
        pltpu.VMEM((TOK, 16 * HD), BF16),
        pltpu.VMEM((TOK, HD), BF16),
        pltpu.VMEM((TOK, HD), BF16),
        pltpu.VMEM((SHARD, HD), BF16),
        pltpu.VMEM((SHARD, HD), BF16),
        pltpu.VMEM((2, 16, HD), BF16),
        pltpu.VMEM((KEYS, HD), BF16),
        pltpu.VMEM((KEYS, 2 * HD), BF16),
        pltpu.VMEM((2, 16 * HD, COLS), BF16),
        pltpu.VMEM((CHUNKS, NY, NZ, rows, L), BF16),
        pltpu.VMEM((CHUNKS, NY, NZ, rows, L), BF16),
        pltpu.VMEM((CHUNKS, NY, TOK, HD), F32),
        pltpu.VMEM((CHUNKS, NY, NZ, rows, L), BF16),
        pltpu.VMEM((CHUNKS, NY, TOK, HD), F32),
        pltpu.VMEM((CHUNKS, NZ, rows, L + HD), BF16),
        pltpu.VMEM((CHUNKS, NZ, rows, L + HD), BF16),
        pltpu.VMEM((CHUNKS, NY, NZ, rows, L), BF16),
        pltpu.VMEM((2, NY * NZ * TOK, COLS), F32),
        pltpu.VMEM((2, NZ, NY * TOK, COLS), BF16),
        pltpu.VMEM((2, NX, NZ // NX, NY * TOK, COLS), BF16),
        dma((8,)),
        dma((4,)),
        dma((4,)),
        dma((CHUNKS, NZ)),
        dma((CHUNKS, NZ)),
        dma((CHUNKS, NY, 1)),
        dma((CHUNKS, NY, 1)),
        dma((CHUNKS, NY)),
        dma((CHUNKS, NY)),
        dma((CHUNKS, NY)),
        dma((CHUNKS, NY)),
        dma((CHUNKS, NY)),
        dma((CHUNKS, NY)),
        dma((CHUNKS, NZ)),
        dma((CHUNKS, NZ)),
        dma((CHUNKS, NZ)),
        dma((CHUNKS, NZ)),
        dma((CHUNKS, NY)),
        dma((CHUNKS, NY)),
        dma((2, NX)),
        dma((2, NX)),
    ]
    return pl.pallas_call(
        kernel,
        out_shape=jax.ShapeDtypeStruct((NZ // NX * NY * 2 * TOK, COLS), BF16),
        in_specs=[hbm, hbm, hbm, sm, sm, hbm, hbm, hbm],
        out_specs=vm,
        scratch_shapes=scratch,
        compiler_params=pltpu.CompilerParams(
            collective_id=0, has_side_effects=True, vmem_limit_bytes=60 << 20
        ),
    )(queries, span_keys, span_values, cache_lengths, span_start, cache_keys, stored_values, out_weight)


def solution(mesh):
    return jax.shard_map(
        device_step,
        mesh=mesh,
        in_specs=(
            P("ctx", "tp"),
            P("ctx", "tp"),
            P("ctx", "tp"),
            P("ctx", "tp"),
            P("ctx", "tp"),
            P("ctx"),
            P(),
            P("tp", "ctx"),
        ),
        out_specs=P("tp", "ctx"),
        check_vma=False,
    )
```

```python
import functools
import math

import jax
import jax.numpy as jnp
from jax import lax
from jax.experimental import pallas as pl
from jax.experimental.pallas import tpu as pltpu
from jax.sharding import PartitionSpec as P

MESH = pl.DeviceIdType.MESH
F32, BF16 = jnp.float32, jnp.bfloat16
NX, NY, NZ, CORES = 4, 4, 8, 2
HD = 128
TOK = 8
SHARD = 1024
CHUNKS = 4
HL = 8 // CHUNKS
L = HL * HD
SPAN_PAD = 128
KEYS = CORES * SHARD + SPAN_PAD
COLS = 256
DEAD = -1e30
SCALE = math.log2(math.e) / math.sqrt(HD)
Y_ORDER = (1, 3, 2)
KB = 512


def nt(a, b):
    return lax.dot_general(a, b, (((1,), (1,)), ((), ())), preferred_element_type=F32)


def nn(a, b):
    return jnp.dot(a, b, preferred_element_type=F32)


def kernel(
    q_ref, sk_ref, sv_ref, len_ref, start_ref, ck_ref, cv_ref, w_ref, out_ref,
    qraw, skraw, svraw, kraw, vraw, span, keys, vals, weight, qg, ob, st, on, sn, nz, nr, ag, terms, tb, tr,
    loc, bar_s, bar_r, qz_s, qz_r, qd_s, qd_r, qy_s, qy_r, ny_s, ny_r, ns_s, ns_r, nz_s, nz_r,
    az_s, az_r, ay_s, ay_r, rx_s, rx_r,
):
    ctx = lax.axis_index("ctx")
    x = lax.axis_index("tp")
    c = ctx % 2
    y = (ctx // 2) % NY
    z = ctx // (2 * NY)
    chip = z * NY + y

    def dev(dx, dy, dz, dc):
        return ((((z + dz % NZ) % NZ) * NY + (y + dy % NY) % NY) * 2 + (c + dc) % 2, (x + dx % NX) % NX)

    def rc(src, dst, ss, rs, to):
        return pltpu.make_async_remote_copy(
            src_ref=src, dst_ref=dst, send_sem=ss, recv_sem=rs, device_id=to, device_id_type=MESH
        )

    peers = [dev(0, 0, 0, 1)]
    peers += [dev(0, d, 0, 0) for d in range(1, NY)]
    peers += [dev(0, 0, d, 0) for d in (4, 3, 5, 2, 6, 1, 7)]
    peers += [dev(d, 0, 0, e) for d in range(1, NX) for e in range(2)]
    barrier = pltpu.get_barrier_semaphore()
    for p in peers:
        pl.semaphore_signal(barrier, inc=1, device_id=p, device_id_type=MESH)

    lk = pltpu.make_async_copy(ck_ref, kraw, loc.at[0])
    lv = pltpu.make_async_copy(cv_ref, vraw, loc.at[1])
    lw = pltpu.make_async_copy(w_ref, weight.at[0], loc.at[2])
    small = [
        pltpu.make_async_copy(a, b, loc.at[3 + i])
        for i, (a, b) in enumerate(
            ((q_ref, qraw), (sk_ref, skraw), (sv_ref, svraw))
        )
    ]
    for cp in small:
        cp.start()
    lk.start()
    lv.start()
    lw.start()

    for cp in small:
        cp.wait()
    qf = qraw[...].astype(F32)
    qf = jnp.concatenate([qf[:, : 8 * HD], qf[:, 8 * HD :]], axis=0).astype(BF16)
    for ci in range(CHUNKS):
        qg[ci, 0, 0] = qf[:, ci * L : (ci + 1) * L]
    span[0] = jnp.concatenate([skraw[...].astype(F32), svraw[...].astype(F32)], axis=0).astype(BF16)

    def qz(ci, d):
        return rc(qg.at[ci, 0, 0], qg.at[ci, 0, d], qz_s.at[ci, d], qz_r.at[ci, d], dev(0, 0, d, 0))

    def qy(ci, d):
        far_z = pl.ds(1, NZ - 1)
        return rc(qg.at[ci, 0, far_z], qg.at[ci, d, far_z], qy_s.at[ci, d], qy_r.at[ci, d], dev(0, d, 0, 0))

    def qd(ci, d, k):
        e = (0, 1, NZ - 1)[k]
        return rc(qg.at[ci, 0, 0], qg.at[ci, d, e], qd_s.at[ci, d, k], qd_r.at[ci, d, k], dev(0, d, e, 0))

    def qy1(d):
        return rc(qg.at[CHUNKS - 1, 0, 0], qg.at[CHUNKS - 1, d, 0], qy_s.at[CHUNKS - 1, d], qy_r.at[CHUNKS - 1, d], dev(0, d, 0, 0))

    def qz1(d):
        return rc(
            qg.at[CHUNKS - 1, :, 0], qg.at[CHUNKS - 1, :, d], qz_s.at[CHUNKS - 1, d], qz_r.at[CHUNKS - 1, d], dev(0, 0, d, 0)
        )

    sib = dev(0, 0, 0, 1)
    own_rows = pl.ds(pl.multiple_of(c * SHARD, SHARD), SHARD)
    csp = rc(span.at[0], span.at[1], bar_s.at[0], bar_r.at[0], sib)
    ck = rc(keys.at[own_rows], keys.at[own_rows], bar_s.at[1], bar_r.at[1], sib)
    cv = rc(vals.at[own_rows], vals.at[own_rows], bar_s.at[2], bar_r.at[2], sib)
    cw = rc(weight.at[0], weight.at[1], bar_s.at[3], bar_r.at[3], sib)
    pl.semaphore_wait(barrier, len(peers))
    last = CHUNKS - 1
    for d in Y_ORDER:
        qy1(d).start()
    for ci in range(last):
        for d in (4, 3, 5, 2, 6, 1, 7):
            qz(ci, d).start()
        for d in Y_ORDER:
            for k in range(1):
                qd(ci, d, k).start()
    csp.start()
    begin = start_ref[0]
    row = lax.broadcasted_iota(jnp.int32, (SHARD, HD), 0)
    live = row < jnp.minimum(len_ref[0], begin - ctx * SHARD)
    lk.wait()
    kr = kraw[...]
    keys[own_rows] = jnp.where(live, kr.astype(F32), kr[0:1].astype(F32)).astype(BF16)
    ck.start()
    lv.wait()
    vals[own_rows, 0:HD] = jnp.where(live, vraw[...].astype(F32), 0.0).astype(BF16)
    vals[own_rows, HD:] = jnp.where(live, 1.0, 0.0).astype(BF16)
    cv.start()
    lw.wait()
    cw.start()
    csp.wait_recv()
    s_own = span[0].astype(F32)
    s_sib = span[1].astype(F32)
    first = jnp.where(c == 0, s_own, s_sib)
    second = jnp.where(c == 0, s_sib, s_own)
    base = CORES * SHARD
    keys[base : base + 16] = jnp.concatenate([first[0:8], second[0:8]], axis=0).astype(BF16)
    keys[base + 16 : KEYS] = jnp.zeros((SPAN_PAD - 16, HD), BF16)
    vals[base : base + 16, 0:HD] = jnp.concatenate([first[8:16], second[8:16]], axis=0).astype(BF16)
    vals[base : base + 16, HD:] = jnp.ones((16, HD), BF16)
    vals[base + 16 : KEYS] = jnp.zeros((SPAN_PAD - 16, 2 * HD), BF16)

    even_live = chip * (2 * SHARD) < begin
    odd_live = chip * (2 * SHARD) + SHARD < begin
    c0 = jnp.where(even_live, SCALE, 0.0).astype(F32)
    b0 = jnp.where(even_live, 0.0, DEAD).astype(F32)
    c1 = jnp.where(odd_live, SCALE, 0.0).astype(F32)
    b1 = jnp.where(odd_live, 0.0, DEAD).astype(F32)
    lane8 = lax.broadcasted_iota(jnp.int32, (TOK, HD), 1)
    lane16 = lax.broadcasted_iota(jnp.int32, (2 * TOK, HD), 1)

    def ny(ci, d, h):
        half = pl.ds(h * (NZ // 2), NZ // 2)
        return rc(ob.at[ci, d, half], on.at[ci, d, half], ny_s.at[ci, d, h], ny_r.at[ci, d, h], dev(0, -d, 0, 0))

    def ns(ci, d):
        return rc(st.at[ci, d], sn.at[ci, d], ns_s.at[ci, d], ns_r.at[ci, d], dev(0, -d, 0, 0))

    def attend(pairs):
        m_rows = len(pairs) * HL * HD
        rows_i = lax.broadcasted_iota(jnp.int32, (HD, SPAN_PAD), 0)
        cols_i = lax.broadcasted_iota(jnp.int32, (HD, SPAN_PAD), 1)
        owner_z = (z + NZ - (rows_i >> 4)) & (NZ - 1)
        blocks, masks = [], []
        for ci, yd in pairs:
            qa = qg[ci, yd]
            token = (owner_z * NY + ((y + NY - yd) & (NY - 1))) * 16 + c * 8 + (rows_i & 7)
            see = (cols_i < 16) & (chip * 16 + cols_i <= token)
            for i in range(HL):
                blocks.append(qa[:, :, i * HD : (i + 1) * HD].reshape(HD, HD))
                masks.append(jnp.where(see, 0.0, 2 * DEAD))
        q2 = jnp.concatenate(blocks, axis=0)
        ss = nt(q2, keys[base:KEYS]) * SCALE + jnp.concatenate(masks, axis=0)
        m = jnp.maximum(jnp.broadcast_to(jnp.max(ss, axis=1, keepdims=True), (m_rows, HD)), DEAD)
        acc = nn(jnp.exp2(ss - m).astype(BF16), vals[base:KEYS])
        for kb in range(0, CORES * SHARD, KB):
            cs, bs = (c0, b0) if kb < SHARD else (c1, b1)
            s = nt(q2, keys[kb : kb + KB])
            top = functools.reduce(jnp.maximum, [s[:, j : j + HD] for j in range(0, KB, HD)])
            top = jnp.broadcast_to(jnp.max(top, axis=1, keepdims=True), (m_rows, HD)) * cs + bs
            new = jnp.maximum(m, top)
            keep = jnp.exp2(m - new)
            off = bs - new
            p = jnp.concatenate(
                [jnp.exp2(s[:, j : j + HD] * cs + off).astype(BF16) for j in range(0, KB, HD)], axis=1
            )
            acc = acc * jnp.concatenate([keep, keep], axis=1) + nn(p, vals[kb : kb + KB])
            m = new
        total = jnp.maximum(acc[:, HD:], 1e-30)
        o = (acc[:, :HD] / total).astype(BF16)
        lse = m + jnp.log2(total)
        for b, (ci, yd) in enumerate(pairs):
            tile = jnp.zeros((TOK, HD), F32)
            for i in range(HL):
                r = (b * HL + i) * HD
                ob[ci, yd, :, :, i * HD : (i + 1) * HD] = o[r : r + HD].reshape(NZ, 16, HD)
                for zd in range(NZ):
                    for hh in range(2):
                        w = r + zd * 16 + hh * 8
                        tile = jnp.where(lane8 == zd * 16 + i * 2 + hh, lse[w : w + 8], tile)
            st[ci, yd] = tile

    def nzc(ci, d):
        return rc(nz.at[ci, d], nr.at[ci, d], nz_s.at[ci, d], nz_r.at[ci, d], dev(0, 0, -d, 0))

    def az(ci, d):
        return rc(ag.at[ci, 0, 0], ag.at[ci, 0, d], az_s.at[ci, d], az_r.at[ci, d], dev(0, 0, d, 0))

    def ay(ci, d):
        return rc(ag.at[ci, 0], ag.at[ci, d], ay_s.at[ci, d], ay_r.at[ci, d], dev(0, d, 0, 0))

    def merge(parts):
        top = functools.reduce(jnp.maximum, [lse for lse, _ in parts])
        ws = [jnp.exp2(lse - top) for lse, _ in parts]
        total = functools.reduce(jnp.add, ws)
        num = functools.reduce(jnp.add, [w * o.astype(F32) for w, (_, o) in zip(ws, parts)])
        return num / total, top + jnp.log2(total)

    def reduce_y(ci):
        for d in range(1, NY):
            ns(ci, d).wait_recv()
        tiles = [st[ci, 0]] + [sn[ci, d] for d in range(1, NY)]
        for zd in (4, 5, 6, 7, 0, 1, 2, 3):
            if zd in (0, NZ // 2):
                for d in range(1, NY):
                    ny(ci, d, zd * 2 // NZ).wait_recv()
            stat = jnp.zeros((16, HD), F32)
            for i in range(HL):
                parts = []
                for d in range(NY):
                    k = zd * 16 + i * 2
                    lse = jnp.concatenate(
                        [jnp.broadcast_to(tiles[d][:, k + hh : k + hh + 1], (8, HD)) for hh in range(2)], axis=0
                    )
                    src = ob if d == 0 else on
                    parts.append((lse, src[ci, d, zd, :, i * HD : (i + 1) * HD]))
                o, lse = merge(parts)
                nz[ci, zd, :, i * HD : (i + 1) * HD] = o.astype(BF16)
                hi = lse.astype(BF16).astype(F32)
                mid = (lse - hi).astype(BF16).astype(F32)
                lo = lse - hi - mid
                for p, v in enumerate((hi, mid, lo)):
                    stat = jnp.where(lane16 == i * 4 + p, v, stat)
            nz[ci, zd, :, L:] = stat.astype(BF16)
            if zd in (3, 7):
                for d in (4, 5, 6, 7) if zd == 7 else (3, 2, 1):
                    nzc(ci, d).start()

    def reduce_z(ci):
        for d in range(1, NZ):
            nzc(ci, d).wait_recv()
        for i in range(HL):
            parts = []
            for d in range(NZ):
                src = nz if d == 0 else nr
                stat = src[ci, d, :, L:].astype(F32)
                pick = (lane16 >= i * 4) & (lane16 < i * 4 + 3)
                lse = jnp.broadcast_to(jnp.sum(jnp.where(pick, stat, 0.0), axis=1, keepdims=True), (16, HD))
                parts.append((lse, src[ci, d, :, i * HD : (i + 1) * HD]))
            o, _ = merge(parts)
            ag[ci, 0, 0, :, i * HD : (i + 1) * HD] = o.astype(BF16)
        for d in (4, 3, 5, 2, 6, 1, 7):
            az(ci, d).start()

    def spread_y(ci):
        for d in range(1, NZ):
            az(ci, d).wait_recv()
        for d in Y_ORDER:
            ay(ci, d).start()

    terms[...] = jnp.zeros_like(terms)

    def project(ci, sides):
        a = ag[ci].astype(F32).reshape(NY * NZ, 16, L)
        for hh in range(2):
            ah = a[:, hh * 8 : (hh + 1) * 8].reshape(NY * NZ * TOK, L).astype(BF16)
            rows = pl.ds(pl.multiple_of(hh * 8 * HD + ci * L, L), L)
            for e in sides:
                terms[e] += nn(ah, weight[e, rows])

    def wait_ay(ci):
        for d in range(1, NY):
            ay(ci, d).wait_recv()

    def send_y(ci, d):
        ns(ci, d).start()
        for h in (1, 0):
            ny(ci, d, h).start()

    def early(t, carry):
        @pl.when(t == 0)
        def _():
            for ci in range(last):
                for d in range(1, NZ):
                    qz(ci, d).wait_recv()
                for d in Y_ORDER:
                    qy(ci, d).start()
                if ci == 0:
                    for d in Y_ORDER:
                        qy1(d).wait_recv()
                    for d in (4, 3, 5, 2, 6, 1, 7):
                        qz1(d).start()
            ck.wait_recv()
            cv.wait_recv()

        @pl.when(t > 0)
        def _():
            for d in Y_ORDER:
                qy(t - 1, d).wait_recv()
                for k in range(1):
                    qd(t - 1, d, k).wait_recv()

        at0 = t == 0
        attend([(jnp.where(at0, i, t - 1), jnp.where(at0, 0, d)) for i, d in enumerate((2, 1, 3))])

        @pl.when(t > 0)
        def _():
            for d in (2, 1, 3):
                send_y(t - 1, d)

        @pl.when(t == CHUNKS - 1)
        def _():
            reduce_y(0)

        return carry

    lax.fori_loop(0, CHUNKS, early, 0)
    for d in range(1, NZ):
        qz1(d).wait_recv()

    def late(t, carry):
        attend([(last, jnp.where(t == 0, a, b)) for a, b in ((2, 3), (1, 0))])

        @pl.when(t == 0)
        def _():
            send_y(last, 2)
            send_y(last, 1)
            reduce_y(1)

        @pl.when(t == 1)
        def _():
            send_y(last, 3)

        return carry

    lax.fori_loop(0, 2, late, 0)
    cw.wait_recv()

    def tail(u, carry):
        @pl.when(u < CHUNKS)
        def _():
            reduce_z(u)

        @pl.when(u < 2)
        def _():
            reduce_y(u + 2)

        @pl.when(u >= 1)
        def _():
            spread_y(u - 1)

        return carry

    lax.fori_loop(0, CHUNKS + 1, tail, 0)

    def drain(ci, carry):
        for d in range(1, NZ):
            qz(ci, d).wait_send()
            nzc(ci, d).wait_send()
            az(ci, d).wait_send()
        for d in range(1, NY):
            qy(ci, d).wait_send()
            for k in range(1):
                qd(ci, d, k).wait_send()
            for h in range(2):
                ny(ci, d, h).wait_send()
            ns(ci, d).wait_send()
        wait_ay(ci)
        project(ci, (0, 1))
        return carry

    lax.fori_loop(0, last, drain, 0)
    for d in range(1, NZ):
        qz1(d).wait_send()
        nzc(last, d).wait_send()
        az(last, d).wait_send()
    for d in range(1, NY):
        qy1(d).wait_send()
        for h in range(2):
            ny(last, d, h).wait_send()
        ns(last, d).wait_send()
    csp.wait_send()
    ck.wait_send()
    cv.wait_send()
    cw.wait_send()
    wait_ay(last)

    ZX = NZ // NX

    def rx(dx, e):
        to = (x + dx) % NX
        return rc(tb.at[e, pl.ds(to * ZX, ZX)], tr.at[e, dx], rx_s.at[e, dx], rx_r.at[e, dx], dev(dx, 0, 0, e))

    for e in (1, 0):
        project(last, (e,))

        def place(zz, carry):
            zd = (z + NZ - zz) % NZ
            parts = []
            for yy in range(NY):
                yd = (y + NY - yy) % NY
                parts.append(terms[e, pl.ds(pl.multiple_of((yd * NZ + zd) * TOK, TOK), TOK)])
            tb[e, zz] = jnp.concatenate(parts, axis=0).astype(BF16)
            return carry

        lax.fori_loop(0, NZ, place, 0)
        for dx in (2, 1, 3):
            rx(dx, e).start()
        if e == 1:
            rx(0, 1).start()
    sums = [tb[0, pl.ds(x * ZX, ZX)].astype(F32), None]
    rx(0, 1).wait_recv()
    sums[1] = tr[1, 0].astype(F32)
    for e in (1, 0):
        for dx in range(1, NX):
            rx(dx, e).wait_recv()
            sums[e] = sums[e] + tr[e, dx].astype(F32)
    low = jnp.where(c == 0, sums[0], sums[1]).reshape(ZX * NY, 1, TOK, COLS)
    high = jnp.where(c == 0, sums[1], sums[0]).reshape(ZX * NY, 1, TOK, COLS)
    out_ref[...] = jnp.concatenate([low, high], axis=1).reshape(ZX * NY * 2 * TOK, COLS).astype(BF16)

    for ci in range(CHUNKS):
        for d in range(1, NY):
            ay(ci, d).wait_send()
    rx(0, 1).wait_send()
    for dx in range(1, NX):
        for e in range(2):
            rx(dx, e).wait_send()


def device_step(queries, span_keys, span_values, cache_keys, stored_values, cache_lengths, span_start, out_weight):
    vm = pl.BlockSpec(memory_space=pltpu.VMEM)
    sm = pl.BlockSpec(memory_space=pltpu.SMEM)
    hbm = pl.BlockSpec(memory_space=pltpu.HBM)
    dma = pltpu.SemaphoreType.DMA
    rows = 16
    scratch = [
        pltpu.VMEM((TOK, 16 * HD), BF16),
        pltpu.VMEM((TOK, HD), BF16),
        pltpu.VMEM((TOK, HD), BF16),
        pltpu.VMEM((SHARD, HD), BF16),
        pltpu.VMEM((SHARD, HD), BF16),
        pltpu.VMEM((2, 16, HD), BF16),
        pltpu.VMEM((KEYS, HD), BF16),
        pltpu.VMEM((KEYS, 2 * HD), BF16),
        pltpu.VMEM((2, 16 * HD, COLS), BF16),
        pltpu.VMEM((CHUNKS, NY, NZ, rows, L), BF16),
        pltpu.VMEM((CHUNKS, NY, NZ, rows, L), BF16),
        pltpu.VMEM((CHUNKS, NY, TOK, HD), F32),
        pltpu.VMEM((CHUNKS, NY, NZ, rows, L), BF16),
        pltpu.VMEM((CHUNKS, NY, TOK, HD), F32),
        pltpu.VMEM((CHUNKS, NZ, rows, L + HD), BF16),
        pltpu.VMEM((CHUNKS, NZ, rows, L + HD), BF16),
        pltpu.VMEM((CHUNKS, NY, NZ, rows, L), BF16),
        pltpu.VMEM((2, NY * NZ * TOK, COLS), F32),
        pltpu.VMEM((2, NZ, NY * TOK, COLS), BF16),
        pltpu.VMEM((2, NX, NZ // NX, NY * TOK, COLS), BF16),
        dma((8,)),
        dma((4,)),
        dma((4,)),
        dma((CHUNKS, NZ)),
        dma((CHUNKS, NZ)),
        dma((CHUNKS, NY, 1)),
        dma((CHUNKS, NY, 1)),
        dma((CHUNKS, NY)),
        dma((CHUNKS, NY)),
        dma((CHUNKS, NY, 2)),
        dma((CHUNKS, NY, 2)),
        dma((CHUNKS, NY)),
        dma((CHUNKS, NY)),
        dma((CHUNKS, NZ)),
        dma((CHUNKS, NZ)),
        dma((CHUNKS, NZ)),
        dma((CHUNKS, NZ)),
        dma((CHUNKS, NY)),
        dma((CHUNKS, NY)),
        dma((2, NX)),
        dma((2, NX)),
    ]
    return pl.pallas_call(
        kernel,
        out_shape=jax.ShapeDtypeStruct((NZ // NX * NY * 2 * TOK, COLS), BF16),
        in_specs=[hbm, hbm, hbm, sm, sm, hbm, hbm, hbm],
        out_specs=vm,
        scratch_shapes=scratch,
        compiler_params=pltpu.CompilerParams(
            collective_id=0, has_side_effects=True, vmem_limit_bytes=60 << 20
        ),
    )(queries, span_keys, span_values, cache_lengths, span_start, cache_keys, stored_values, out_weight)


def solution(mesh):
    return jax.shard_map(
        device_step,
        mesh=mesh,
        in_specs=(
            P("ctx", "tp"),
            P("ctx", "tp"),
            P("ctx", "tp"),
            P("ctx", "tp"),
            P("ctx", "tp"),
            P("ctx"),
            P(),
            P("tp", "ctx"),
        ),
        out_specs=P("tp", "ctx"),
        check_vma=False,
    )
```

```python
import functools
import math

import jax
import jax.numpy as jnp
from jax import lax
from jax.experimental import pallas as pl
from jax.experimental.pallas import tpu as pltpu
from jax.sharding import PartitionSpec as P

MESH = pl.DeviceIdType.MESH
F32, BF16 = jnp.float32, jnp.bfloat16
NX, NY, NZ, CORES = 4, 4, 8, 2
HD = 128
TOK = 8
SHARD = 1024
CHUNKS = 4
HL = 8 // CHUNKS
L = HL * HD
SPAN_PAD = 128
KEYS = CORES * SHARD + SPAN_PAD
COLS = 256
DEAD = -1e30
SCALE = math.log2(math.e) / math.sqrt(HD)
Y_ORDER = (1, 3, 2)
KB = 512


def nt(a, b):
    return lax.dot_general(a, b, (((1,), (1,)), ((), ())), preferred_element_type=F32)


def nn(a, b):
    return jnp.dot(a, b, preferred_element_type=F32)


def kernel(
    q_ref, sk_ref, sv_ref, len_ref, start_ref, ck_ref, cv_ref, w_ref, out_ref,
    qraw, skraw, svraw, kraw, vraw, span, keys, vals, weight, qg, ob, st, on, sn, nz, nr, ag, terms, tb, tr,
    loc, bar_s, bar_r, qz_s, qz_r, qd_s, qd_r, qy_s, qy_r, ny_s, ny_r, ns_s, ns_r, nz_s, nz_r,
    az_s, az_r, ay_s, ay_r, rx_s, rx_r,
):
    ctx = lax.axis_index("ctx")
    x = lax.axis_index("tp")
    c = ctx % 2
    y = (ctx // 2) % NY
    z = ctx // (2 * NY)
    chip = z * NY + y

    def dev(dx, dy, dz, dc):
        return ((((z + dz % NZ) % NZ) * NY + (y + dy % NY) % NY) * 2 + (c + dc) % 2, (x + dx % NX) % NX)

    def rc(src, dst, ss, rs, to):
        return pltpu.make_async_remote_copy(
            src_ref=src, dst_ref=dst, send_sem=ss, recv_sem=rs, device_id=to, device_id_type=MESH
        )

    peers = [dev(0, 0, 0, 1)]
    peers += [dev(0, d, 0, 0) for d in range(1, NY)]
    peers += [dev(0, 0, d, 0) for d in (4, 3, 5, 2, 6, 1, 7)]
    peers += [dev(d, 0, 0, e) for d in range(1, NX) for e in range(2)]
    barrier = pltpu.get_barrier_semaphore()
    for p in peers:
        pl.semaphore_signal(barrier, inc=1, device_id=p, device_id_type=MESH)

    lk = pltpu.make_async_copy(ck_ref, kraw, loc.at[0])
    lv = pltpu.make_async_copy(cv_ref, vraw, loc.at[1])
    lw = pltpu.make_async_copy(w_ref, weight.at[0], loc.at[2])
    small = [
        pltpu.make_async_copy(a, b, loc.at[3 + i])
        for i, (a, b) in enumerate(
            ((q_ref, qraw), (sk_ref, skraw), (sv_ref, svraw))
        )
    ]
    for cp in small:
        cp.start()
    lk.start()
    lv.start()
    lw.start()

    for cp in small:
        cp.wait()
    qf = qraw[...].astype(F32)
    qf = jnp.concatenate([qf[:, : 8 * HD], qf[:, 8 * HD :]], axis=0).astype(BF16)
    for ci in range(CHUNKS):
        qg[ci, 0, 0] = qf[:, ci * L : (ci + 1) * L]
    span[0] = jnp.concatenate([skraw[...].astype(F32), svraw[...].astype(F32)], axis=0).astype(BF16)

    def qz(ci, d):
        return rc(qg.at[ci, 0, 0], qg.at[ci, 0, d], qz_s.at[ci, d], qz_r.at[ci, d], dev(0, 0, d, 0))

    def qy(ci, d):
        far_z = pl.ds(1, NZ - 1)
        return rc(qg.at[ci, 0, far_z], qg.at[ci, d, far_z], qy_s.at[ci, d], qy_r.at[ci, d], dev(0, d, 0, 0))

    def qd(ci, d, k):
        e = (0, 1, NZ - 1)[k]
        return rc(qg.at[ci, 0, 0], qg.at[ci, d, e], qd_s.at[ci, d, k], qd_r.at[ci, d, k], dev(0, d, e, 0))

    def qy1(d):
        return rc(qg.at[CHUNKS - 1, 0, 0], qg.at[CHUNKS - 1, d, 0], qy_s.at[CHUNKS - 1, d], qy_r.at[CHUNKS - 1, d], dev(0, d, 0, 0))

    def qz1(d):
        return rc(
            qg.at[CHUNKS - 1, :, 0], qg.at[CHUNKS - 1, :, d], qz_s.at[CHUNKS - 1, d], qz_r.at[CHUNKS - 1, d], dev(0, 0, d, 0)
        )

    sib = dev(0, 0, 0, 1)
    own_rows = pl.ds(pl.multiple_of(c * SHARD, SHARD), SHARD)
    csp = rc(span.at[0], span.at[1], bar_s.at[0], bar_r.at[0], sib)
    ck = rc(keys.at[own_rows], keys.at[own_rows], bar_s.at[1], bar_r.at[1], sib)
    cv = rc(vals.at[own_rows], vals.at[own_rows], bar_s.at[2], bar_r.at[2], sib)
    cw = rc(weight.at[0], weight.at[1], bar_s.at[3], bar_r.at[3], sib)
    pl.semaphore_wait(barrier, len(peers))
    last = CHUNKS - 1
    for d in Y_ORDER:
        qy1(d).start()
    for ci in range(last):
        for d in (4, 3, 5, 2, 6, 1, 7):
            qz(ci, d).start()
        for d in Y_ORDER:
            for k in range(1):
                qd(ci, d, k).start()
    csp.start()
    begin = start_ref[0]
    row = lax.broadcasted_iota(jnp.int32, (SHARD, HD), 0)
    live = row < jnp.minimum(len_ref[0], begin - ctx * SHARD)
    lk.wait()
    kr = kraw[...]
    keys[own_rows] = jnp.where(live, kr.astype(F32), kr[0:1].astype(F32)).astype(BF16)
    ck.start()
    lv.wait()
    vals[own_rows, 0:HD] = jnp.where(live, vraw[...].astype(F32), 0.0).astype(BF16)
    vals[own_rows, HD:] = jnp.where(live, 1.0, 0.0).astype(BF16)
    cv.start()
    lw.wait()
    cw.start()
    csp.wait_recv()
    s_own = span[0].astype(F32)
    s_sib = span[1].astype(F32)
    first = jnp.where(c == 0, s_own, s_sib)
    second = jnp.where(c == 0, s_sib, s_own)
    base = CORES * SHARD
    keys[base : base + 16] = jnp.concatenate([first[0:8], second[0:8]], axis=0).astype(BF16)
    keys[base + 16 : KEYS] = jnp.zeros((SPAN_PAD - 16, HD), BF16)
    vals[base : base + 16, 0:HD] = jnp.concatenate([first[8:16], second[8:16]], axis=0).astype(BF16)
    vals[base : base + 16, HD:] = jnp.ones((16, HD), BF16)
    vals[base + 16 : KEYS] = jnp.zeros((SPAN_PAD - 16, 2 * HD), BF16)

    even_live = chip * (2 * SHARD) < begin
    odd_live = chip * (2 * SHARD) + SHARD < begin
    c0 = jnp.where(even_live, SCALE, 0.0).astype(F32)
    b0 = jnp.where(even_live, 0.0, DEAD).astype(F32)
    c1 = jnp.where(odd_live, SCALE, 0.0).astype(F32)
    b1 = jnp.where(odd_live, 0.0, DEAD).astype(F32)
    lane8 = lax.broadcasted_iota(jnp.int32, (TOK, HD), 1)
    lane16 = lax.broadcasted_iota(jnp.int32, (2 * TOK, HD), 1)

    def ny(ci, d):
        return rc(ob.at[ci, d], on.at[ci, d], ny_s.at[ci, d], ny_r.at[ci, d], dev(0, -d, 0, 0))

    def ns(ci, d):
        return rc(st.at[ci, d], sn.at[ci, d], ns_s.at[ci, d], ns_r.at[ci, d], dev(0, -d, 0, 0))

    def attend(pairs):
        m_rows = len(pairs) * HL * HD
        rows_i = lax.broadcasted_iota(jnp.int32, (HD, SPAN_PAD), 0)
        cols_i = lax.broadcasted_iota(jnp.int32, (HD, SPAN_PAD), 1)
        owner_z = (z + NZ - (rows_i >> 4)) & (NZ - 1)
        blocks, masks = [], []
        for ci, yd in pairs:
            qa = qg[ci, yd]
            token = (owner_z * NY + ((y + NY - yd) & (NY - 1))) * 16 + c * 8 + (rows_i & 7)
            see = (cols_i < 16) & (chip * 16 + cols_i <= token)
            for i in range(HL):
                blocks.append(qa[:, :, i * HD : (i + 1) * HD].reshape(HD, HD))
                masks.append(jnp.where(see, 0.0, 2 * DEAD))
        q2 = jnp.concatenate(blocks, axis=0)
        ss = nt(q2, keys[base:KEYS]) * SCALE + jnp.concatenate(masks, axis=0)
        m = jnp.maximum(jnp.broadcast_to(jnp.max(ss, axis=1, keepdims=True), (m_rows, HD)), DEAD)
        acc = nn(jnp.exp2(ss - m).astype(BF16), vals[base:KEYS])
        for kb in range(0, CORES * SHARD, KB):
            cs, bs = (c0, b0) if kb < SHARD else (c1, b1)
            s = nt(q2, keys[kb : kb + KB])
            top = functools.reduce(jnp.maximum, [s[:, j : j + HD] for j in range(0, KB, HD)])
            top = jnp.broadcast_to(jnp.max(top, axis=1, keepdims=True), (m_rows, HD)) * cs + bs
            new = jnp.maximum(m, top)
            keep = jnp.exp2(m - new)
            off = bs - new
            p = jnp.concatenate(
                [jnp.exp2(s[:, j : j + HD] * cs + off).astype(BF16) for j in range(0, KB, HD)], axis=1
            )
            acc = acc * jnp.concatenate([keep, keep], axis=1) + nn(p, vals[kb : kb + KB])
            m = new
        total = jnp.maximum(acc[:, HD:], 1e-30)
        o = (acc[:, :HD] / total).astype(BF16)
        lse = m + jnp.log2(total)
        for b, (ci, yd) in enumerate(pairs):
            tile = jnp.zeros((TOK, HD), F32)
            for i in range(HL):
                r = (b * HL + i) * HD
                ob[ci, yd, :, :, i * HD : (i + 1) * HD] = o[r : r + HD].reshape(NZ, 16, HD)
                for zd in range(NZ):
                    for hh in range(2):
                        w = r + zd * 16 + hh * 8
                        tile = jnp.where(lane8 == zd * 16 + i * 2 + hh, lse[w : w + 8], tile)
            st[ci, yd] = tile

    def nzc(ci, d):
        return rc(nz.at[ci, d], nr.at[ci, d], nz_s.at[ci, d], nz_r.at[ci, d], dev(0, 0, -d, 0))

    def az(ci, d):
        return rc(ag.at[ci, 0, 0], ag.at[ci, 0, d], az_s.at[ci, d], az_r.at[ci, d], dev(0, 0, d, 0))

    def ay(ci, d):
        return rc(ag.at[ci, 0], ag.at[ci, d], ay_s.at[ci, d], ay_r.at[ci, d], dev(0, d, 0, 0))

    def merge(parts):
        top = functools.reduce(jnp.maximum, [lse for lse, _ in parts])
        ws = [jnp.exp2(lse - top) for lse, _ in parts]
        total = functools.reduce(jnp.add, ws)
        num = functools.reduce(jnp.add, [w * o.astype(F32) for w, (_, o) in zip(ws, parts)])
        return num / total, top + jnp.log2(total)

    def reduce_y(ci):
        for d in range(1, NY):
            ny(ci, d).wait_recv()
            ns(ci, d).wait_recv()
        tiles = [st[ci, 0]] + [sn[ci, d] for d in range(1, NY)]
        for zd in range(NZ):
            stat = jnp.zeros((16, HD), F32)
            for i in range(HL):
                parts = []
                for d in range(NY):
                    k = zd * 16 + i * 2
                    lse = jnp.concatenate(
                        [jnp.broadcast_to(tiles[d][:, k + hh : k + hh + 1], (8, HD)) for hh in range(2)], axis=0
                    )
                    src = ob if d == 0 else on
                    parts.append((lse, src[ci, d, zd, :, i * HD : (i + 1) * HD]))
                o, lse = merge(parts)
                nz[ci, zd, :, i * HD : (i + 1) * HD] = o.astype(BF16)
                hi = lse.astype(BF16).astype(F32)
                mid = (lse - hi).astype(BF16).astype(F32)
                lo = lse - hi - mid
                for p, v in enumerate((hi, mid, lo)):
                    stat = jnp.where(lane16 == i * 4 + p, v, stat)
            nz[ci, zd, :, L:] = stat.astype(BF16)
        for d in (4, 3, 5, 2, 6, 1, 7):
            nzc(ci, d).start()

    def reduce_z(ci):
        for d in range(1, NZ):
            nzc(ci, d).wait_recv()
        for i in range(HL):
            parts = []
            for d in range(NZ):
                src = nz if d == 0 else nr
                stat = src[ci, d, :, L:].astype(F32)
                pick = (lane16 >= i * 4) & (lane16 < i * 4 + 3)
                lse = jnp.broadcast_to(jnp.sum(jnp.where(pick, stat, 0.0), axis=1, keepdims=True), (16, HD))
                parts.append((lse, src[ci, d, :, i * HD : (i + 1) * HD]))
            o, _ = merge(parts)
            ag[ci, 0, 0, :, i * HD : (i + 1) * HD] = o.astype(BF16)
        for d in (4, 3, 5, 2, 6, 1, 7):
            az(ci, d).start()

    def spread_y(ci):
        for d in range(1, NZ):
            az(ci, d).wait_recv()
        for d in Y_ORDER:
            ay(ci, d).start()

    terms[...] = jnp.zeros_like(terms)

    def project(ci, sides):
        a = ag[ci].astype(F32).reshape(NY * NZ, 16, L)
        for hh in range(2):
            ah = a[:, hh * 8 : (hh + 1) * 8].reshape(NY * NZ * TOK, L).astype(BF16)
            rows = pl.ds(pl.multiple_of(hh * 8 * HD + ci * L, L), L)
            for e in sides:
                terms[e] += nn(ah, weight[e, rows])

    def wait_ay(ci):
        for d in range(1, NY):
            ay(ci, d).wait_recv()

    def send_y(ci, d):
        ny(ci, d).start()
        ns(ci, d).start()

    def early(t, carry):
        @pl.when(t == 0)
        def _():
            for ci in range(last):
                for d in range(1, NZ):
                    qz(ci, d).wait_recv()
                for d in Y_ORDER:
                    qy(ci, d).start()
                if ci == 0:
                    for d in Y_ORDER:
                        qy1(d).wait_recv()
                    for d in (4, 3, 5, 2, 6, 1, 7):
                        qz1(d).start()
            ck.wait_recv()
            cv.wait_recv()

        @pl.when(t > 0)
        def _():
            for d in Y_ORDER:
                qy(t - 1, d).wait_recv()
                for k in range(1):
                    qd(t - 1, d, k).wait_recv()

        at0 = t == 0
        attend([(jnp.where(at0, i, t - 1), jnp.where(at0, 0, d)) for i, d in enumerate((2, 1, 3))])

        @pl.when(t > 0)
        def _():
            for d in (2, 1, 3):
                send_y(t - 1, d)

        @pl.when(t == CHUNKS - 1)
        def _():
            reduce_y(0)

        return carry

    lax.fori_loop(0, CHUNKS, early, 0)
    for d in range(1, NZ):
        qz1(d).wait_recv()

    def late(t, carry):
        attend([(last, jnp.where(t == 0, a, b)) for a, b in ((2, 3), (1, 0))])

        @pl.when(t == 0)
        def _():
            send_y(last, 2)
            send_y(last, 1)
            reduce_y(1)

        @pl.when(t == 1)
        def _():
            send_y(last, 3)

        return carry

    lax.fori_loop(0, 2, late, 0)
    cw.wait_recv()

    def tail(u, carry):
        @pl.when(u >= 2)
        def _():
            spread_y(u - 2)

        @pl.when(u < CHUNKS)
        def _():
            reduce_z(u)

        @pl.when(u == CHUNKS)
        def _():
            spread_y(u - 1)

        @pl.when(u < 2)
        def _():
            reduce_y(u + 2)

        return carry

    lax.fori_loop(0, CHUNKS + 1, tail, 0)

    def drain(ci, carry):
        for d in range(1, NZ):
            qz(ci, d).wait_send()
            nzc(ci, d).wait_send()
            az(ci, d).wait_send()
        for d in range(1, NY):
            qy(ci, d).wait_send()
            for k in range(1):
                qd(ci, d, k).wait_send()
            ny(ci, d).wait_send()
            ns(ci, d).wait_send()
        wait_ay(ci)
        project(ci, (0, 1))
        return carry

    lax.fori_loop(0, last, drain, 0)
    for d in range(1, NZ):
        qz1(d).wait_send()
        nzc(last, d).wait_send()
        az(last, d).wait_send()
    for d in range(1, NY):
        qy1(d).wait_send()
        ny(last, d).wait_send()
        ns(last, d).wait_send()
    csp.wait_send()
    ck.wait_send()
    cv.wait_send()
    cw.wait_send()
    wait_ay(last)

    ZX = NZ // NX

    def rx(dx, e):
        to = (x + dx) % NX
        return rc(tb.at[e, pl.ds(to * ZX, ZX)], tr.at[e, dx], rx_s.at[e, dx], rx_r.at[e, dx], dev(dx, 0, 0, e))

    for e in (1, 0):
        project(last, (e,))

        def place(zz, carry):
            zd = (z + NZ - zz) % NZ
            parts = []
            for yy in range(NY):
                yd = (y + NY - yy) % NY
                parts.append(terms[e, pl.ds(pl.multiple_of((yd * NZ + zd) * TOK, TOK), TOK)])
            tb[e, zz] = jnp.concatenate(parts, axis=0).astype(BF16)
            return carry

        lax.fori_loop(0, NZ, place, 0)
        for dx in (2, 1, 3):
            rx(dx, e).start()
        if e == 1:
            rx(0, 1).start()
    sums = [tb[0, pl.ds(x * ZX, ZX)].astype(F32), None]
    rx(0, 1).wait_recv()
    sums[1] = tr[1, 0].astype(F32)
    for e in (1, 0):
        for dx in range(1, NX):
            rx(dx, e).wait_recv()
            sums[e] = sums[e] + tr[e, dx].astype(F32)
    low = jnp.where(c == 0, sums[0], sums[1]).reshape(ZX * NY, 1, TOK, COLS)
    high = jnp.where(c == 0, sums[1], sums[0]).reshape(ZX * NY, 1, TOK, COLS)
    out_ref[...] = jnp.concatenate([low, high], axis=1).reshape(ZX * NY * 2 * TOK, COLS).astype(BF16)

    for ci in range(CHUNKS):
        for d in range(1, NY):
            ay(ci, d).wait_send()
    rx(0, 1).wait_send()
    for dx in range(1, NX):
        for e in range(2):
            rx(dx, e).wait_send()


def device_step(queries, span_keys, span_values, cache_keys, stored_values, cache_lengths, span_start, out_weight):
    vm = pl.BlockSpec(memory_space=pltpu.VMEM)
    sm = pl.BlockSpec(memory_space=pltpu.SMEM)
    hbm = pl.BlockSpec(memory_space=pltpu.HBM)
    dma = pltpu.SemaphoreType.DMA
    rows = 16
    scratch = [
        pltpu.VMEM((TOK, 16 * HD), BF16),
        pltpu.VMEM((TOK, HD), BF16),
        pltpu.VMEM((TOK, HD), BF16),
        pltpu.VMEM((SHARD, HD), BF16),
        pltpu.VMEM((SHARD, HD), BF16),
        pltpu.VMEM((2, 16, HD), BF16),
        pltpu.VMEM((KEYS, HD), BF16),
        pltpu.VMEM((KEYS, 2 * HD), BF16),
        pltpu.VMEM((2, 16 * HD, COLS), BF16),
        pltpu.VMEM((CHUNKS, NY, NZ, rows, L), BF16),
        pltpu.VMEM((CHUNKS, NY, NZ, rows, L), BF16),
        pltpu.VMEM((CHUNKS, NY, TOK, HD), F32),
        pltpu.VMEM((CHUNKS, NY, NZ, rows, L), BF16),
        pltpu.VMEM((CHUNKS, NY, TOK, HD), F32),
        pltpu.VMEM((CHUNKS, NZ, rows, L + HD), BF16),
        pltpu.VMEM((CHUNKS, NZ, rows, L + HD), BF16),
        pltpu.VMEM((CHUNKS, NY, NZ, rows, L), BF16),
        pltpu.VMEM((2, NY * NZ * TOK, COLS), F32),
        pltpu.VMEM((2, NZ, NY * TOK, COLS), BF16),
        pltpu.VMEM((2, NX, NZ // NX, NY * TOK, COLS), BF16),
        dma((8,)),
        dma((4,)),
        dma((4,)),
        dma((CHUNKS, NZ)),
        dma((CHUNKS, NZ)),
        dma((CHUNKS, NY, 1)),
        dma((CHUNKS, NY, 1)),
        dma((CHUNKS, NY)),
        dma((CHUNKS, NY)),
        dma((CHUNKS, NY)),
        dma((CHUNKS, NY)),
        dma((CHUNKS, NY)),
        dma((CHUNKS, NY)),
        dma((CHUNKS, NZ)),
        dma((CHUNKS, NZ)),
        dma((CHUNKS, NZ)),
        dma((CHUNKS, NZ)),
        dma((CHUNKS, NY)),
        dma((CHUNKS, NY)),
        dma((2, NX)),
        dma((2, NX)),
    ]
    return pl.pallas_call(
        kernel,
        out_shape=jax.ShapeDtypeStruct((NZ // NX * NY * 2 * TOK, COLS), BF16),
        in_specs=[hbm, hbm, hbm, sm, sm, hbm, hbm, hbm],
        out_specs=vm,
        scratch_shapes=scratch,
        compiler_params=pltpu.CompilerParams(
            collective_id=0, has_side_effects=True, vmem_limit_bytes=60 << 20
        ),
    )(queries, span_keys, span_values, cache_lengths, span_start, cache_keys, stored_values, out_weight)


def solution(mesh):
    return jax.shard_map(
        device_step,
        mesh=mesh,
        in_specs=(
            P("ctx", "tp"),
            P("ctx", "tp"),
            P("ctx", "tp"),
            P("ctx", "tp"),
            P("ctx", "tp"),
            P("ctx"),
            P(),
            P("tp", "ctx"),
        ),
        out_specs=P("tp", "ctx"),
        check_vma=False,
    )
```
